32 devices in a mesh: row: 8 (over y, x, core), col: 4 (over z).
Axes of the slice: x: 2, y: 2, z: 4, core: 2. Of those that a mesh axis runs over, the one named last changes fastest.
Arguments:
- matrix: float32 [1536, 1536], P('row', 'col'), as said below
- left_panel: float32 [1536, 1024], P('row', 'col'), may hold values from -2.5 to 2.5
- right_panel: float32 [1536, 1024], P('row', 'col'), may hold values from -2.5 to 2.5
- reflectors: float32 [1536, 256], P('row', 'col'), may hold values from -0.3125 to 0.3125
Outputs:
- updated: float32 [1536, 1536], P('row', 'col')
The draws below stay inside these ranges and needn't reach their ends.
Inputs may be any that keep to these rules, and one draw needn't show every extreme that they name: matrix is exactly skew-symmetric.
All inputs are finite; a program needn't handle non-finite values.
Results may differ from the reference program's by a relative error of at most 0.00011.
Values sent between devices are 32-bit elements; how exact they have to be, the bound alone decides.
No kernel may reach another device: no remote copies, remote signals or barrier semaphores. Data moves between devices by JAX's collectives and lax.ppermute only.
A program may use at most 128 MiB of HBM per device.

```python
import jax
import jax.numpy as jnp
from jax import lax

NB = 256
N = 1536
K = 1024


def draw_matrix(key, part):
    normal_part = jax.random.normal(jax.random.fold_in(key, 11), (N, N), jnp.float32)
    return (normal_part - normal_part.T) * 0.7071


def block_levels(stream_key, dims, shards, low, top_value):
    level = 1.0
    for axis_at, parts in shards:
        steps = jax.random.uniform(jax.random.fold_in(jax.random.fold_in(stream_key, 6), axis_at), (parts,), jnp.float32, low / len(shards), top_value / len(shards))
        level = level * jnp.repeat(jnp.exp(steps), dims[axis_at] // parts).reshape((-1,) + (1,) * (len(dims) - 1 - axis_at))
    return level


def noise(key, extent, scale, bound, pieces=(), kind=jnp.bfloat16):
    gain = block_levels(key, extent, pieces, -0.22, 0.18) if pieces else 1.0
    drawn = jax.random.normal(key, extent, jnp.float32) * scale * gain
    return jnp.minimum(jnp.maximum(drawn, -bound), bound).astype(kind)


def setup_inputs(seed: int = 0) -> dict:
    arg_keys = jax.random.split(jax.random.key(seed), 5)
    matrix = draw_matrix(jax.random.fold_in(arg_keys[4], 71), 0)
    left_panel = noise(arg_keys[1], (N, K), (K ** -0.25), 2.5, ((0, 8), (1, 4)), jnp.float32)
    right_panel = noise(arg_keys[2], (N, K), (K ** -0.25), 2.5, ((0, 8), (1, 4)), jnp.float32)
    reflectors = noise(arg_keys[3], (N, NB), (N // 4) ** -0.5, 0.3125, ((0, 8), (1, 4)), jnp.float32)
    return {"matrix": matrix, "left_panel": left_panel, "right_panel": right_panel, "reflectors": reflectors}


def product(first, second):
    return jnp.dot(first, second, precision=lax.Precision.HIGHEST, preferred_element_type=jnp.float32)


def reference(matrix, left_panel, right_panel, reflectors):
    reduced = matrix - product(left_panel, right_panel.T) + product(right_panel, left_panel.T)
    image = product(reduced, reflectors)
    return reduced + product(reflectors, image.T) - product(image, reflectors.T)
```

```python
import jax
import jax.numpy as jnp
from jax import lax
from jax.sharding import PartitionSpec as P


def dot(first, second, dims):
    return lax.dot_general(
        first,
        second,
        (dims, ((), ())),
        precision=lax.Precision.HIGH,
        preferred_element_type=jnp.float32,
    )


def swap(value, axis, offset):
    size = lax.axis_size(axis)
    return lax.ppermute(value, axis, [(i, i ^ offset) for i in range(size)])


def gather_rows(value, rows):
    own = {0: value}
    for chip in range(2, rows, 2):
        own[chip] = swap(value, "row", chip)
    blocks = []
    for chip in range(0, rows, 2):
        blocks += [own[chip], swap(own[chip], "row", 1)]
    return jnp.concatenate(blocks, axis=0)


def sum_rows(value, rows):
    core = lax.axis_index("row") % 2
    half = value.shape[0] // 2
    kept = lax.dynamic_slice_in_dim(value, core * half, half, 0)
    given = lax.dynamic_slice_in_dim(value, (1 - core) * half, half, 0)
    total = kept + swap(given, "row", 1)
    bit = 2
    while bit < rows:
        total = total + swap(total, "row", bit)
        bit *= 2
    other = swap(total, "row", 1)
    first = jnp.where(core == 0, total, other)
    second = jnp.where(core == 0, other, total)
    return jnp.concatenate([first, second], axis=0)


def order_blocks(value, per, first):
    width = value.shape[1] // per
    bit = 1
    while bit < per:
        parts = [value[:, t * width : (t + 1) * width] for t in range(per)]
        moved = jnp.concatenate([parts[t ^ bit] for t in range(per)], axis=1)
        value = jnp.where((first // bit) % 2 == 1, moved, value)
        bit *= 2
    return value


def local(matrix, left_panel, right_panel, reflectors):
    rows, cols = lax.axis_size("row"), lax.axis_size("col")
    per = rows // cols
    row, col = lax.axis_index("row"), lax.axis_index("col")
    height, share = left_panel.shape
    wide = per * height

    own_refl = jnp.concatenate(
        [reflectors] + [swap(reflectors, "col", k) for k in range(1, cols)], axis=1
    )
    panels = jnp.concatenate([left_panel, right_panel], axis=1)
    all_panels = gather_rows(panels, rows)
    all_refl = gather_rows(own_refl, rows)

    def start(offset):
        return ((row // per) ^ col ^ offset) * wide

    along = ((1,), (1,))
    over = ((1,), (0,))
    mixed = dot(all_panels, all_refl, ((0,), (0,)))
    mixed_left, mixed_right = mixed[:share], mixed[share:]
    mine = order_blocks(matrix, per, row % per)
    col_refl = lax.dynamic_slice_in_dim(all_refl, start(0), wide, 0)
    image = (
        dot(right_panel, mixed_left, over)
        - dot(left_panel, mixed_right, over)
        + dot(mine, col_refl, over)
    )
    factors = jnp.concatenate(
        [
            right_panel - dot(own_refl, mixed_right, along),
            dot(own_refl, mixed_left, along) - left_panel,
            -image,
        ],
        axis=1,
    )
    whole = jnp.concatenate([all_panels, all_refl], axis=1)

    def block(offset):
        return dot(factors, lax.dynamic_slice_in_dim(whole, start(offset), wide, 0), along)

    total = block(0)
    for k in range(1, cols):
        total = total + swap(block(k), "col", k)
    sides = sum_rows(dot(own_refl, matrix, ((0,), (0,))), rows)
    return order_blocks(total, per, row % per) + (matrix - dot(own_refl, sides, over))


def solution(mesh):
    spec = P("row", "col")
    return jax.shard_map(
        local, mesh=mesh, in_specs=(spec,) * 4, out_specs=spec, check_vma=False
    )
```

```python
import functools

import jax
import jax.numpy as jnp
from jax import lax
from jax.experimental import pallas as pl
from jax.experimental.pallas import tpu as pltpu
from jax.sharding import PartitionSpec as P

ALONG = ((1,), (1,))
OVER = ((1,), (0,))
DOWN = ((0,), (0,))
VMEM_BYTES = 24 * 2**20


def dot(first, second, dims):
    return lax.dot_general(
        first,
        second,
        (dims, ((), ())),
        precision=lax.Precision.HIGH,
        preferred_element_type=jnp.float32,
    )


def halves(value):
    high = value.astype(jnp.bfloat16)
    return high, (value - high.astype(jnp.float32)).astype(jnp.bfloat16)


def pair_dot(first, second, dims):
    def one(a, b):
        return lax.dot_general(a, b, (dims, ((), ())), preferred_element_type=jnp.float32)

    return one(first[0], second[0]) + (one(first[0], second[1]) + one(first[1], second[0]))


def swap(value, axis, offset):
    size = lax.axis_size(axis)
    return lax.ppermute(value, axis, [(i, i ^ offset) for i in range(size)])


def gather_row(value, rows):
    blocks = []
    for chip in range(0, rows, 2):
        here = swap(value, "row", chip) if chip else value
        blocks += [here, swap(here, "row", 1)]
    return blocks


def stack(*parts):
    return jnp.concatenate(parts, axis=0)


def gather_square(panels, own_refl, height):
    near_x, near_y = swap(panels, "row", 2), swap(panels, "row", 4)
    by_x = swap(stack(near_y[:height], own_refl), "row", 2)
    by_y = swap(stack(near_x[height:], own_refl), "row", 4)
    far = swap(own_refl, "row", 6)
    found = []
    for value, places in (
        (panels, ((0, 0), (0, 1))),
        (near_x, ((2, 0), (2, 1))),
        (near_y, ((4, 0), (4, 1))),
        (own_refl, ((0, 2),)),
        (by_x, ((6, 0), (2, 2))),
        (by_y, ((6, 1), (4, 2))),
        (far, ((6, 2),)),
    ):
        found.append((value, places))
        found.append((swap(value, "row", 1), tuple((i + 1, kind) for i, kind in places)))
    return found


def core_sum(value):
    core = lax.axis_index("row") % 2
    half = value.shape[0] // 2
    kept = lax.dynamic_slice_in_dim(value, core * half, half, 0)
    given = lax.dynamic_slice_in_dim(value, (1 - core) * half, half, 0)
    return kept + swap(given, "row", 1)


def chips_sum(total, rows):
    bit = 2
    while bit < rows:
        total = total + swap(total, "row", bit)
        bit *= 2
    core = lax.axis_index("row") % 2
    other = swap(total, "row", 1)
    first = jnp.where(core == 0, total, other)
    second = jnp.where(core == 0, other, total)
    return jnp.concatenate([first, second], axis=0)


def order_blocks(value, per, first):
    width = value.shape[1] // per
    bit = 1
    while bit < per:
        parts = [value[:, t * width : (t + 1) * width] for t in range(per)]
        moved = jnp.concatenate([parts[t ^ bit] for t in range(per)], axis=1)
        value = jnp.where((first // bit) % 2 == 1, moved, value)
        bit *= 2
    return value


def block_kernel(pieces, cols, per, share, place, *refs):
    in_refs, matrix = refs[: len(pieces)], refs[len(pieces)]
    outs = refs[len(pieces) + 1 : len(pieces) + 1 + cols]
    high, low, made = refs[len(pieces) + 1 + cols :]
    height = matrix.shape[0]
    wide = per * height
    base, first = place[0], place[1]
    for ref, places in zip(in_refs, pieces):
        for n, (index, kind) in enumerate(places):
            upper, lower = halves(ref[n * height : (n + 1) * height, :])
            rows = slice(index * height, (index + 1) * height)
            columns = slice(kind * share, kind * share + ref.shape[1])
            high[rows, columns] = upper
            low[rows, columns] = lower
    panels = (high[:, : 2 * share], low[:, : 2 * share])
    refl = (high[:, 2 * share :], low[:, 2 * share :])
    mixed = pair_dot(refl, panels, DOWN)
    own = in_refs[0][...]
    left_panel, right_panel = own[:height], own[height:]
    mixed_pair = halves(mixed)
    own_refl = (high[:height, 2 * share :], low[:height, 2 * share :])
    spread = pair_dot(own_refl, mixed_pair, OVER)
    turned = halves(jnp.concatenate([right_panel, -left_panel], axis=1))
    image = pair_dot(turned, mixed_pair, ALONG)
    for t in range(per):
        begin = pl.multiple_of((base * per + (t ^ first)) * height, 16)
        rows = pl.ds(begin, height)
        image = image + pair_dot(
            halves(matrix[:, t * height : (t + 1) * height]),
            (high[rows, 2 * share :], low[rows, 2 * share :]),
            OVER,
        )
    factors = halves(
        jnp.concatenate(
            [right_panel - spread[:, share:], spread[:, :share] - left_panel, -image], axis=1
        )
    )
    for block in range(cols):
        rows = slice(block * wide, (block + 1) * wide)
        made[block] = pair_dot(factors, (high[rows, :], low[rows, :]), ALONG)
    for k in range(cols):
        outs[k][...] = made[base ^ k]


def blocks_in_kernel(found, matrix, place, rows, cols, share, width):
    per = rows // cols
    arrays = [value for value, _ in found]
    pieces = tuple(places for _, places in found)
    height = matrix.shape[0]
    total, depth = rows * height, 2 * share + width
    out = jax.ShapeDtypeStruct((height, per * height), jnp.float32)
    flops = 6 * total * (2 * share * width + height * depth)
    vmem = pl.BlockSpec(memory_space=pltpu.VMEM)
    return pl.pallas_call(
        functools.partial(block_kernel, pieces, cols, per, share),
        out_shape=[out] * cols,
        in_specs=[pl.BlockSpec(memory_space=pltpu.SMEM)] + [vmem] * (len(arrays) + 1),
        out_specs=[vmem] * cols,
        scratch_shapes=[
            pltpu.VMEM((total, depth), jnp.bfloat16),
            pltpu.VMEM((total, depth), jnp.bfloat16),
            pltpu.VMEM((cols, height, per * height), jnp.float32),
        ],
        compiler_params=pltpu.CompilerParams(vmem_limit_bytes=VMEM_BYTES),
        cost_estimate=pl.CostEstimate(
            flops=flops, bytes_accessed=4 * total * depth, transcendentals=0
        ),
    )(place, *arrays, matrix)


def blocks_plain(panels, refls, matrix, base, first, cols, per):
    all_panels, all_refl = jnp.concatenate(panels, axis=0), jnp.concatenate(refls, axis=0)
    own, own_refl = panels[0], refls[0]
    height, share = own.shape[0], own.shape[1] // 2
    wide = per * height
    left_panel, right_panel = own[:, :share], own[:, share:]
    mixed = dot(all_panels, all_refl, DOWN)
    mixed_left, mixed_right = mixed[:share], mixed[share:]
    mine = order_blocks(matrix, per, first)
    col_refl = lax.dynamic_slice_in_dim(all_refl, base * wide, wide, 0)
    image = (
        dot(right_panel, mixed_left, OVER)
        - dot(left_panel, mixed_right, OVER)
        + dot(mine, col_refl, OVER)
    )
    factors = jnp.concatenate(
        [
            right_panel - dot(own_refl, mixed_right, ALONG),
            dot(own_refl, mixed_left, ALONG) - left_panel,
            -image,
        ],
        axis=1,
    )
    whole = jnp.concatenate([all_panels, all_refl], axis=1)
    return [
        dot(factors, lax.dynamic_slice_in_dim(whole, (base ^ k) * wide, wide, 0), ALONG)
        for k in range(cols)
    ]


def local(matrix, left_panel, right_panel, reflectors):
    rows, cols = lax.axis_size("row"), lax.axis_size("col")
    per = rows // cols
    row, col = lax.axis_index("row"), lax.axis_index("col")
    height, share = left_panel.shape
    base, first = (row // per) ^ col, row % per

    own_refl = reflectors
    bit = 1
    while bit < cols:
        own_refl = jnp.concatenate([own_refl, swap(own_refl, "col", bit)], axis=1)
        bit *= 2
    width = own_refl.shape[1]
    halved = core_sum(dot(own_refl, matrix, DOWN))

    need = rows * height * (2 * share + width) * 8 + rows * height * height * 8
    if rows == 8 and share == width and need <= VMEM_BYTES:
        found = gather_square(stack(left_panel, right_panel), own_refl, height)
        place = jnp.stack([base, first]).astype(jnp.int32)
        made = blocks_in_kernel(found, matrix, place, rows, cols, share, width)
    else:
        panels = gather_row(jnp.concatenate([left_panel, right_panel], axis=1), rows)
        refls = gather_row(own_refl, rows)
        made = blocks_plain(panels, refls, matrix, base, first, cols, per)

    halved, own_refl, _ = lax.optimization_barrier((halved, own_refl, made[0]))
    received = [swap(made[k], "col", k) for k in range(1, cols)]
    rest = lax.optimization_barrier(matrix - dot(own_refl, chips_sum(halved, rows), OVER))
    total = made[0]
    for block in received:
        total = total + block
    return order_blocks(total, per, first) + rest


def solution(mesh):
    spec = P("row", "col")
    return jax.shard_map(
        local, mesh=mesh, in_specs=(spec,) * 4, out_specs=spec, check_vma=False
    )
```

```python
import functools

import jax
import jax.numpy as jnp
from jax import lax
from jax.experimental import pallas as pl
from jax.experimental.pallas import tpu as pltpu
from jax.sharding import PartitionSpec as P

ALONG = ((1,), (1,))
OVER = ((1,), (0,))
DOWN = ((0,), (0,))
VMEM_BYTES = 24 * 2**20


def dot(first, second, dims):
    return lax.dot_general(
        first,
        second,
        (dims, ((), ())),
        precision=lax.Precision.HIGH,
        preferred_element_type=jnp.float32,
    )


def halves(value):
    high = value.astype(jnp.bfloat16)
    return high, (value - high.astype(jnp.float32)).astype(jnp.bfloat16)


def pair_dot(first, second, dims):
    def one(a, b):
        return lax.dot_general(a, b, (dims, ((), ())), preferred_element_type=jnp.float32)

    return one(first[0], second[0]) + (one(first[0], second[1]) + one(first[1], second[0]))


def swap(value, axis, offset):
    size = lax.axis_size(axis)
    return lax.ppermute(value, axis, [(i, i ^ offset) for i in range(size)])


def gather_row(value, rows):
    blocks = []
    for chip in range(0, rows, 2):
        here = swap(value, "row", chip) if chip else value
        blocks += [here, swap(here, "row", 1)]
    return blocks


def stack(*parts):
    return jnp.concatenate(parts, axis=0)


def pack_kernel(panels, near_x, near_y, *refs):
    *parts, by_x, by_y, near = refs
    height = panels.shape[0] // 2
    at = 0
    for part in parts:
        near[:height, at : at + part.shape[1]] = part[...]
        at += part.shape[1]
    for n, value in enumerate((panels, near_x, near_y)):
        near[(2 * n + 1) * height : (2 * n + 3) * height, :] = value[...]
    by_x[:height, :] = near_y[:height, :]
    by_x[height:, :] = near[:height, :]
    by_y[:height, :] = near_x[height:, :]
    by_y[height:, :] = near[:height, :]


def gather_square(panels, refl_parts, height):
    near_x, near_y = swap(panels, "row", 2), swap(panels, "row", 4)
    width = panels.shape[1]
    by_x, by_y, near = run_kernel(
        pack_kernel,
        [(2 * height, width)] * 2 + [(7 * height, width)],
        [panels, near_x, near_y, *refl_parts],
        (),
        0,
        72 * height * width,
    )
    far = swap(near[:height], "row", 6)
    by_x, by_y = swap(by_x, "row", 2), swap(by_y, "row", 4)
    last = stack(by_x, by_y, far)
    near_at = ((0, 2), (0, 0), (0, 1), (2, 0), (2, 1), (4, 0), (4, 1))
    last_at = ((6, 0), (2, 2), (6, 1), (4, 2), (6, 2))

    def across(places):
        return tuple((index + 1, kind) for index, kind in places)

    found = []
    for value, places in ((near, near_at), (last, last_at)):
        found += [(value, places), (swap(value, "row", 1), across(places))]
    return found, near, by_x


def core_sum(value):
    core = lax.axis_index("row") % 2
    half = value.shape[0] // 2
    kept = lax.dynamic_slice_in_dim(value, core * half, half, 0)
    given = lax.dynamic_slice_in_dim(value, (1 - core) * half, half, 0)
    return kept + swap(given, "row", 1)


def chips_sum(total, rows):
    bit = 2
    while bit < rows:
        total = total + swap(total, "row", bit)
        bit *= 2
    core = lax.axis_index("row") % 2
    other = swap(total, "row", 1)
    first = jnp.where(core == 0, total, other)
    second = jnp.where(core == 0, other, total)
    return jnp.concatenate([first, second], axis=0)


def order_blocks(value, per, first):
    width = value.shape[1] // per
    bit = 1
    while bit < per:
        parts = [value[:, t * width : (t + 1) * width] for t in range(per)]
        moved = jnp.concatenate([parts[t ^ bit] for t in range(per)], axis=1)
        value = jnp.where((first // bit) % 2 == 1, moved, value)
        bit *= 2
    return value


def place_in_kernel(per):
    row, col = lax.axis_index("row"), lax.axis_index("col")
    return (row // per) ^ col, row % per


def split_pieces(pieces, in_refs, high, low, height, share):
    for ref, places in zip(in_refs, pieces):
        for n, (index, kind) in enumerate(places):
            upper, lower = halves(ref[n * height : (n + 1) * height, :])
            rows = slice(index * height, (index + 1) * height)
            columns = slice(kind * share, (kind + 1) * share)
            high[rows, columns] = upper
            low[rows, columns] = lower


def block_of(factors, high, low, begin, wide):
    height = factors.shape[0] // 2
    rows = pl.ds(pl.multiple_of(begin, 16), wide)

    def one(a, b):
        return lax.dot_general(a, b, (ALONG, ((), ())), preferred_element_type=jnp.float32)

    both = one(factors, high[rows, :])
    return both[:height] + (both[height:] + one(factors[:height], low[rows, :]))


def send_kernel(pieces, per, share, offsets, *refs):
    count = len(pieces)
    in_refs, matrix, factors_ref = refs[:count], refs[count], refs[count + 1]
    outs = refs[count + 2 : count + 2 + len(offsets)]
    high, low = refs[count + 2 + len(offsets) :]
    height = matrix.shape[0]
    wide = per * height
    base, first = place_in_kernel(per)
    split_pieces(pieces, in_refs, high, low, height, share)
    panels = (high[:, : 2 * share], low[:, : 2 * share])
    refl = (high[:, 2 * share :], low[:, 2 * share :])
    mixed_pair = halves(pair_dot(refl, panels, DOWN))
    left_panel, right_panel = (in_refs[0][n * height : (n + 1) * height, :] for n in (1, 2))
    own_refl = (high[:height, 2 * share :], low[:height, 2 * share :])
    spread = pair_dot(own_refl, mixed_pair, OVER)
    turned = halves(jnp.concatenate([right_panel, -left_panel], axis=1))
    image = pair_dot(turned, mixed_pair, ALONG)
    for t in range(per):
        begin = pl.multiple_of((base * per + (t ^ first)) * height, 16)
        rows = pl.ds(begin, height)
        image = image + pair_dot(
            halves(matrix[:, t * height : (t + 1) * height]),
            (high[rows, 2 * share :], low[rows, 2 * share :]),
            OVER,
        )
    factors = jnp.concatenate(
        [right_panel - spread[:, share:], spread[:, :share] - left_panel, -image], axis=1
    )
    factors_ref[...] = factors
    stacked = jnp.concatenate(halves(factors), axis=0)
    for k, out in zip(offsets, outs):
        out[...] = block_of(stacked, high, low, (base ^ k) * wide, wide)


def keep_kernel(pieces, per, share, *refs):
    count = len(pieces)
    in_refs, (factors_ref, matrix, out, high, low, made) = refs[:count], refs[count:]
    height = matrix.shape[0]
    wide = per * height
    base, first = place_in_kernel(per)
    split_pieces(pieces, in_refs, high, low, height, share)
    stacked = jnp.concatenate(halves(factors_ref[...]), axis=0)
    made[...] = block_of(stacked, high, low, base * wide, wide)
    put_in_order(out, matrix, made, first, per)


def put_in_order(out, base, total, first, per):
    height = out.shape[0]
    for other in range(per):

        @pl.when(first == other)
        def _():
            for t in range(per):
                here = slice(t * height, (t + 1) * height)
                there = slice((t ^ other) * height, ((t ^ other) + 1) * height)
                out[:, here] = base[:, here] + total[:, there]


def sides_kernel(near, matrix, out):
    refl = near[: matrix.shape[0], :]
    out[...] = pair_dot(halves(refl), halves(matrix[...]), DOWN)


def sum_kernel(per, *refs):
    *blocks, base, out, made = refs
    _, first = place_in_kernel(per)
    total = blocks[0][...]
    for block in blocks[1:]:
        total = total + block[...]
    made[...] = total
    put_in_order(out, base, made, first, per)


def last_kernel(*refs):
    summed, sides, *parts, near, out = refs
    refl = near[: out.shape[0], :]
    whole = sides[...] + jnp.concatenate([part[...] for part in parts], axis=0)
    out[...] = summed[...] - pair_dot(halves(refl), halves(whole), OVER)


def run_kernel(body, outs, args, scratch=(), flops=0, moved=0):
    vmem = pl.BlockSpec(memory_space=pltpu.VMEM)
    return pl.pallas_call(
        body,
        out_shape=[jax.ShapeDtypeStruct(shape, jnp.float32) for shape in outs],
        in_specs=[vmem] * len(args),
        out_specs=[vmem] * len(outs),
        scratch_shapes=list(scratch),
        compiler_params=pltpu.CompilerParams(vmem_limit_bytes=VMEM_BYTES),
        cost_estimate=pl.CostEstimate(flops=flops, bytes_accessed=moved, transcendentals=0),
    )(*args)


def blocks_plain(panels, refls, matrix, base, first, cols, per):
    all_panels, all_refl = jnp.concatenate(panels, axis=0), jnp.concatenate(refls, axis=0)
    own, own_refl = panels[0], refls[0]
    height, share = own.shape[0], own.shape[1] // 2
    wide = per * height
    left_panel, right_panel = own[:, :share], own[:, share:]
    mixed = dot(all_panels, all_refl, DOWN)
    mixed_left, mixed_right = mixed[:share], mixed[share:]
    mine = order_blocks(matrix, per, first)
    col_refl = lax.dynamic_slice_in_dim(all_refl, base * wide, wide, 0)
    image = (
        dot(right_panel, mixed_left, OVER)
        - dot(left_panel, mixed_right, OVER)
        + dot(mine, col_refl, OVER)
    )
    factors = jnp.concatenate(
        [
            right_panel - dot(own_refl, mixed_right, ALONG),
            dot(own_refl, mixed_left, ALONG) - left_panel,
            -image,
        ],
        axis=1,
    )
    whole = jnp.concatenate([all_panels, all_refl], axis=1)
    return [
        dot(factors, lax.dynamic_slice_in_dim(whole, (base ^ k) * wide, wide, 0), ALONG)
        for k in range(cols)
    ]


def gather_columns(reflectors, cols):
    value, bit = reflectors, 1
    while bit < cols:
        value = jnp.concatenate([value, swap(value, "col", bit)], axis=1)
        bit *= 2
    return value


def local_square(matrix, left_panel, right_panel, reflectors):
    rows, cols = lax.axis_size("row"), lax.axis_size("col")
    per = rows // cols
    height, share = left_panel.shape
    wide = per * height
    refl_parts, bit = [reflectors], 1
    while bit < cols:
        known = jnp.concatenate(refl_parts, axis=1)
        refl_parts = [known, swap(known, "col", bit)]
        bit *= 2
    found, near, by_x = gather_square(stack(left_panel, right_panel), refl_parts, height)
    width = share
    (sides,) = run_kernel(
        sides_kernel,
        [(width, wide)],
        [near, matrix],
        (),
        6 * height * width * wide,
        4 * height * (width + wide),
    )
    sides = sides + swap(sides, "row", 1)
    sides, _ = lax.optimization_barrier((sides, by_x))
    beside = swap(sides, "row", 2)

    arrays = [value for value, _ in found]
    pieces = tuple(places for _, places in found)
    total, depth = rows * height, 2 * share + width
    halved = pltpu.VMEM((total, depth), jnp.bfloat16)
    block = pltpu.VMEM((height, wide), jnp.float32)
    offsets = sorted(range(1, cols), key=lambda k: (k == 1, k))
    factors, *blocks = run_kernel(
        functools.partial(send_kernel, pieces, per, share, offsets),
        [(height, depth)] + [(height, wide)] * len(offsets),
        arrays + [matrix],
        [halved, halved],
        12 * total * share * width + 6 * total * height * depth,
        4 * total * depth,
    )
    received = [swap(b, "col", k) for k, b in zip(offsets, blocks)]
    (base,) = run_kernel(
        functools.partial(keep_kernel, pieces, per, share),
        [(height, wide)],
        arrays + [factors, matrix],
        [halved, halved, block],
        6 * wide * height * depth,
        4 * total * depth,
    )
    sides, beside, _ = lax.optimization_barrier((sides, beside, factors))
    sides = sides + beside
    parts = [swap(sides[n : n + width // 2], "row", 4) for n in (0, width // 2)]
    (summed,) = run_kernel(
        functools.partial(sum_kernel, per),
        [(height, wide)],
        [*received, base],
        [block],
        height * wide * cols,
        4 * height * wide * (cols + 1),
    )
    summed, parts = lax.optimization_barrier((summed, parts))
    (updated,) = run_kernel(
        last_kernel,
        [(height, wide)],
        [summed, sides, *parts, near],
        (),
        6 * height * width * wide,
        4 * width * wide * 2,
    )
    return updated


def local_general(matrix, left_panel, right_panel, reflectors):
    rows, cols = lax.axis_size("row"), lax.axis_size("col")
    per = rows // cols
    row, col = lax.axis_index("row"), lax.axis_index("col")
    base, first = (row // per) ^ col, row % per
    own_refl = gather_columns(reflectors, cols)
    panels = gather_row(jnp.concatenate([left_panel, right_panel], axis=1), rows)
    refls = gather_row(own_refl, rows)
    made = blocks_plain(panels, refls, matrix, base, first, cols, per)
    total = made[0]
    for k in range(1, cols):
        total = total + swap(made[k], "col", k)
    sides = chips_sum(core_sum(dot(own_refl, matrix, DOWN)), rows)
    return order_blocks(total, per, first) + (matrix - dot(own_refl, sides, OVER))


def local(matrix, left_panel, right_panel, reflectors):
    rows, cols = lax.axis_size("row"), lax.axis_size("col")
    height, share = left_panel.shape
    width = reflectors.shape[1] * cols
    need = rows * height * (2 * share + width) * 8 + rows * height * height * 8
    if rows == 8 and share == width and need <= VMEM_BYTES:
        return local_square(matrix, left_panel, right_panel, reflectors)
    return local_general(matrix, left_panel, right_panel, reflectors)


def solution(mesh):
    spec = P("row", "col")
    return jax.shard_map(
        local, mesh=mesh, in_specs=(spec,) * 4, out_specs=spec, check_vma=False
    )
```

```python
import functools

import jax
import jax.numpy as jnp
from jax import lax
from jax.experimental import pallas as pl
from jax.experimental.pallas import tpu as pltpu
from jax.sharding import PartitionSpec as P

ALONG = ((1,), (1,))
OVER = ((1,), (0,))
DOWN = ((0,), (0,))
VMEM_BYTES = 24 * 2**20


def dot(first, second, dims):
    return lax.dot_general(
        first,
        second,
        (dims, ((), ())),
        precision=lax.Precision.HIGH,
        preferred_element_type=jnp.float32,
    )


def halves(value):
    high = value.astype(jnp.bfloat16)
    return high, (value - high.astype(jnp.float32)).astype(jnp.bfloat16)


def pair_dot(first, second, dims):
    def one(a, b):
        return lax.dot_general(a, b, (dims, ((), ())), preferred_element_type=jnp.float32)

    return one(first[0], second[0]) + (one(first[0], second[1]) + one(first[1], second[0]))


def swap(value, axis, offset):
    size = lax.axis_size(axis)
    return lax.ppermute(value, axis, [(i, i ^ offset) for i in range(size)])


def gather_row(value, rows):
    blocks = []
    for chip in range(0, rows, 2):
        here = swap(value, "row", chip) if chip else value
        blocks += [here, swap(here, "row", 1)]
    return blocks


def stack(*parts):
    return jnp.concatenate(parts, axis=0)


def pack_kernel(left_x, right_x, left_y, right_y, *refs):
    *parts, by_x, by_y, near = refs
    height = left_x.shape[0]
    near[:height, :] = jnp.concatenate([part[...] for part in parts], axis=0).T
    for n, value in enumerate((left_x, right_x, left_y, right_y)):
        near[(n + 1) * height : (n + 2) * height, :] = value[...]
    by_x[:height, :] = left_y[...]
    by_x[height:, :] = near[:height, :]
    by_y[:height, :] = right_x[...]
    by_y[height:, :] = near[:height, :]


def gather_square(left_panel, right_panel, refl_parts, matrix):
    height, width = left_panel.shape
    wide = matrix.shape[1]
    near = [swap(panel, "row", bits) for bits in (2, 4) for panel in (left_panel, right_panel)]
    by_x, by_y, near = run_kernel(
        pack_kernel,
        [(2 * height, width)] * 2 + [(5 * height, width)],
        [*near, *refl_parts],
        (),
        0,
        72 * height * width,
    )
    far = swap(near[:height], "row", 6)
    by_x, by_y = swap(by_x, "row", 2), swap(by_y, "row", 4)
    (sides,) = run_kernel(
        sides_kernel,
        [(width, wide)],
        [near, matrix],
        (),
        6 * height * width * wide,
        4 * height * (width + wide),
    )
    sides = sides + swap(sides, "row", 1)
    panels = stack(left_panel, right_panel)
    across_own = swap(panels, "row", 1)
    last, across_own = lax.optimization_barrier((stack(by_x, by_y, far), across_own))
    own_at = ((0, 0), (0, 1))
    near_at = ((0, 2), (2, 0), (2, 1), (4, 0), (4, 1))
    last_at = ((6, 0), (2, 2), (6, 1), (4, 2), (6, 2))

    def across(places):
        return tuple((index + 1, kind) for index, kind in places)

    found = [(panels, own_at), (across_own, across(own_at))]
    for value, places in ((near, near_at), (last, last_at)):
        found += [(value, places), (swap(value, "row", 1), across(places))]
    return found, near, sides, by_x


def core_sum(value):
    core = lax.axis_index("row") % 2
    half = value.shape[0] // 2
    kept = lax.dynamic_slice_in_dim(value, core * half, half, 0)
    given = lax.dynamic_slice_in_dim(value, (1 - core) * half, half, 0)
    return kept + swap(given, "row", 1)


def chips_sum(total, rows):
    bit = 2
    while bit < rows:
        total = total + swap(total, "row", bit)
        bit *= 2
    core = lax.axis_index("row") % 2
    other = swap(total, "row", 1)
    first = jnp.where(core == 0, total, other)
    second = jnp.where(core == 0, other, total)
    return jnp.concatenate([first, second], axis=0)


def order_blocks(value, per, first):
    width = value.shape[1] // per
    bit = 1
    while bit < per:
        parts = [value[:, t * width : (t + 1) * width] for t in range(per)]
        moved = jnp.concatenate([parts[t ^ bit] for t in range(per)], axis=1)
        value = jnp.where((first // bit) % 2 == 1, moved, value)
        bit *= 2
    return value


def place_in_kernel(per):
    row, col = lax.axis_index("row"), lax.axis_index("col")
    return (row // per) ^ col, row % per


def split_pieces(pieces, in_refs, high, low, height, share):
    for ref, places in zip(in_refs, pieces):
        for n, (index, kind) in enumerate(places):
            upper, lower = halves(ref[n * height : (n + 1) * height, :])
            rows = slice(index * height, (index + 1) * height)
            columns = slice(kind * share, (kind + 1) * share)
            high[rows, columns] = upper
            low[rows, columns] = lower


def block_of(factors, high, low, begin, wide):
    height = factors.shape[0] // 2
    rows = pl.ds(pl.multiple_of(begin, 16), wide)

    def one(a, b):
        return lax.dot_general(a, b, (ALONG, ((), ())), preferred_element_type=jnp.float32)

    both = one(factors, high[rows, :])
    return both[:height] + (both[height:] + one(factors[:height], low[rows, :]))


def send_kernel(pieces, per, share, offsets, *refs):
    count = len(pieces)
    in_refs, matrix, factors_ref = refs[:count], refs[count], refs[count + 1]
    outs = refs[count + 2 : count + 2 + len(offsets)]
    high, low = refs[count + 2 + len(offsets) :]
    height = matrix.shape[0]
    wide = per * height
    base, first = place_in_kernel(per)
    split_pieces(pieces, in_refs, high, low, height, share)
    panels = (high[:, : 2 * share], low[:, : 2 * share])
    refl = (high[:, 2 * share :], low[:, 2 * share :])
    mixed_pair = halves(pair_dot(refl, panels, DOWN))
    left_panel, right_panel = in_refs[0][:height, :], in_refs[0][height:, :]
    own_refl = (high[:height, 2 * share :], low[:height, 2 * share :])
    spread = pair_dot(own_refl, mixed_pair, OVER)
    turned = halves(jnp.concatenate([right_panel, -left_panel], axis=1))
    image = pair_dot(turned, mixed_pair, ALONG)
    for t in range(per):
        begin = pl.multiple_of((base * per + (t ^ first)) * height, 16)
        rows = pl.ds(begin, height)
        image = image + pair_dot(
            halves(matrix[:, t * height : (t + 1) * height]),
            (high[rows, 2 * share :], low[rows, 2 * share :]),
            OVER,
        )
    factors = jnp.concatenate(
        [right_panel - spread[:, share:], spread[:, :share] - left_panel, -image], axis=1
    )
    factors_ref[...] = factors
    stacked = jnp.concatenate(halves(factors), axis=0)
    for k, out in zip(offsets, outs):
        out[...] = block_of(stacked, high, low, (base ^ k) * wide, wide)


def keep_kernel(pieces, per, share, *refs):
    count = len(pieces)
    in_refs, (factors_ref, matrix, out, high, low, made) = refs[:count], refs[count:]
    height = matrix.shape[0]
    wide = per * height
    base, first = place_in_kernel(per)
    split_pieces(pieces, in_refs, high, low, height, share)
    stacked = jnp.concatenate(halves(factors_ref[...]), axis=0)
    made[...] = block_of(stacked, high, low, base * wide, wide)
    put_in_order(out, matrix, made, first, per)


def put_in_order(out, base, total, first, per):
    height = out.shape[0]
    for other in range(per):

        @pl.when(first == other)
        def _():
            for t in range(per):
                here = slice(t * height, (t + 1) * height)
                there = slice((t ^ other) * height, ((t ^ other) + 1) * height)
                out[:, here] = base[:, here] + total[:, there]


def sides_kernel(near, matrix, out):
    refl = near[: matrix.shape[0], :]
    out[...] = pair_dot(halves(refl), halves(matrix[...]), DOWN)


def sum_kernel(per, *refs):
    *blocks, base, out, made = refs
    _, first = place_in_kernel(per)
    total = blocks[0][...]
    for block in blocks[1:]:
        total = total + block[...]
    made[...] = total
    put_in_order(out, base, made, first, per)


def last_kernel(*refs):
    summed, sides, *parts, near, out = refs
    refl = near[: out.shape[0], :]
    whole = sides[...] + jnp.concatenate([part[...] for part in parts], axis=0)
    out[...] = summed[...] - pair_dot(halves(refl), halves(whole), OVER)


def run_kernel(body, outs, args, scratch=(), flops=0, moved=0):
    vmem = pl.BlockSpec(memory_space=pltpu.VMEM)
    return pl.pallas_call(
        body,
        out_shape=[jax.ShapeDtypeStruct(shape, jnp.float32) for shape in outs],
        in_specs=[vmem] * len(args),
        out_specs=[vmem] * len(outs),
        scratch_shapes=list(scratch),
        compiler_params=pltpu.CompilerParams(vmem_limit_bytes=VMEM_BYTES),
        cost_estimate=pl.CostEstimate(flops=flops, bytes_accessed=moved, transcendentals=0),
    )(*args)


def blocks_plain(panels, refls, matrix, base, first, cols, per):
    all_panels, all_refl = jnp.concatenate(panels, axis=0), jnp.concatenate(refls, axis=0)
    own, own_refl = panels[0], refls[0]
    height, share = own.shape[0], own.shape[1] // 2
    wide = per * height
    left_panel, right_panel = own[:, :share], own[:, share:]
    mixed = dot(all_panels, all_refl, DOWN)
    mixed_left, mixed_right = mixed[:share], mixed[share:]
    mine = order_blocks(matrix, per, first)
    col_refl = lax.dynamic_slice_in_dim(all_refl, base * wide, wide, 0)
    image = (
        dot(right_panel, mixed_left, OVER)
        - dot(left_panel, mixed_right, OVER)
        + dot(mine, col_refl, OVER)
    )
    factors = jnp.concatenate(
        [
            right_panel - dot(own_refl, mixed_right, ALONG),
            dot(own_refl, mixed_left, ALONG) - left_panel,
            -image,
        ],
        axis=1,
    )
    whole = jnp.concatenate([all_panels, all_refl], axis=1)
    return [
        dot(factors, lax.dynamic_slice_in_dim(whole, (base ^ k) * wide, wide, 0), ALONG)
        for k in range(cols)
    ]


def gather_columns(reflectors, cols):
    value, bit = reflectors, 1
    while bit < cols:
        value = jnp.concatenate([value, swap(value, "col", bit)], axis=1)
        bit *= 2
    return value


def local_square(matrix, left_panel, right_panel, reflectors):
    rows, cols = lax.axis_size("row"), lax.axis_size("col")
    per = rows // cols
    height, share = left_panel.shape
    wide = per * height
    refl_parts, bit = [reflectors.T], 1
    while bit < cols:
        known = jnp.concatenate(refl_parts, axis=0)
        refl_parts = [known, swap(known, "col", bit)]
        bit *= 2
    found, near, sides, by_x = gather_square(left_panel, right_panel, refl_parts, matrix)
    width = share
    sides, _ = lax.optimization_barrier((sides, by_x))
    beside = swap(sides, "row", 2)

    arrays = [value for value, _ in found]
    pieces = tuple(places for _, places in found)
    total, depth = rows * height, 2 * share + width
    halved = pltpu.VMEM((total, depth), jnp.bfloat16)
    block = pltpu.VMEM((height, wide), jnp.float32)
    offsets = sorted(range(1, cols), key=lambda k: (k == 1, k))
    factors, *blocks = run_kernel(
        functools.partial(send_kernel, pieces, per, share, offsets),
        [(height, depth)] + [(height, wide)] * len(offsets),
        arrays + [matrix],
        [halved, halved],
        12 * total * share * width + 6 * total * height * depth,
        4 * total * depth,
    )
    received = [swap(b, "col", k) for k, b in zip(offsets, blocks)]
    (base,) = run_kernel(
        functools.partial(keep_kernel, pieces, per, share),
        [(height, wide)],
        arrays + [factors, matrix],
        [halved, halved, block],
        6 * wide * height * depth,
        4 * total * depth,
    )
    sides, beside, _ = lax.optimization_barrier((sides, beside, factors))
    sides = sides + beside
    parts = [swap(sides[n : n + width // 2], "row", 4) for n in (0, width // 2)]
    (summed,) = run_kernel(
        functools.partial(sum_kernel, per),
        [(height, wide)],
        [*received, base],
        [block],
        height * wide * cols,
        16 * height * wide * (cols + 1),
    )
    summed, parts = lax.optimization_barrier((summed, parts))
    (updated,) = run_kernel(
        last_kernel,
        [(height, wide)],
        [summed, sides, *parts, near],
        (),
        6 * height * width * wide,
        4 * width * wide * 2,
    )
    return updated


def local_general(matrix, left_panel, right_panel, reflectors):
    rows, cols = lax.axis_size("row"), lax.axis_size("col")
    per = rows // cols
    row, col = lax.axis_index("row"), lax.axis_index("col")
    base, first = (row // per) ^ col, row % per
    own_refl = gather_columns(reflectors, cols)
    panels = gather_row(jnp.concatenate([left_panel, right_panel], axis=1), rows)
    refls = gather_row(own_refl, rows)
    made = blocks_plain(panels, refls, matrix, base, first, cols, per)
    total = made[0]
    for k in range(1, cols):
        total = total + swap(made[k], "col", k)
    sides = chips_sum(core_sum(dot(own_refl, matrix, DOWN)), rows)
    return order_blocks(total, per, first) + (matrix - dot(own_refl, sides, OVER))


def local(matrix, left_panel, right_panel, reflectors):
    rows, cols = lax.axis_size("row"), lax.axis_size("col")
    height, share = left_panel.shape
    width = reflectors.shape[1] * cols
    need = rows * height * (2 * share + width) * 8 + rows * height * height * 8
    if rows == 8 and share == width and need <= VMEM_BYTES:
        return local_square(matrix, left_panel, right_panel, reflectors)
    return local_general(matrix, left_panel, right_panel, reflectors)


def solution(mesh):
    spec = P("row", "col")
    return jax.shard_map(
        local, mesh=mesh, in_specs=(spec,) * 4, out_specs=spec, check_vma=False
    )
```

```python
import functools

import jax
import jax.numpy as jnp
from jax import lax
from jax.experimental import pallas as pl
from jax.experimental.pallas import tpu as pltpu
from jax.sharding import PartitionSpec as P

ALONG = ((1,), (1,))
OVER = ((1,), (0,))
DOWN = ((0,), (0,))
VMEM_BYTES = 24 * 2**20


def dot(first, second, dims):
    return lax.dot_general(
        first,
        second,
        (dims, ((), ())),
        precision=lax.Precision.HIGH,
        preferred_element_type=jnp.float32,
    )


def halves(value):
    high = value.astype(jnp.bfloat16)
    return high, (value - high.astype(jnp.float32)).astype(jnp.bfloat16)


def pair_dot(first, second, dims):
    def one(a, b):
        return lax.dot_general(a, b, (dims, ((), ())), preferred_element_type=jnp.float32)

    return one(first[0], second[0]) + (one(first[0], second[1]) + one(first[1], second[0]))


def swap(value, axis, offset):
    size = lax.axis_size(axis)
    return lax.ppermute(value, axis, [(i, i ^ offset) for i in range(size)])


def gather_row(value, rows):
    blocks = []
    for chip in range(0, rows, 2):
        here = swap(value, "row", chip) if chip else value
        blocks += [here, swap(here, "row", 1)]
    return blocks


def stack(*parts):
    return jnp.concatenate(parts, axis=0)


def pack_kernel(left_x, right_x, left_y, right_y, *refs):
    *parts, by_x, by_y, near = refs
    height = left_x.shape[0]
    near[:height, :] = jnp.concatenate([part[...] for part in parts], axis=0).T
    for n, value in enumerate((left_x, right_x, left_y, right_y)):
        near[(n + 1) * height : (n + 2) * height, :] = value[...]
    by_x[:height, :] = left_y[...]
    by_x[height:, :] = near[:height, :]
    by_y[:height, :] = right_x[...]
    by_y[height:, :] = near[:height, :]


def gather_square(left_panel, right_panel, refl_parts, matrix):
    height, width = left_panel.shape
    wide = matrix.shape[1]
    near = [swap(panel, "row", bits) for bits in (2, 4) for panel in (left_panel, right_panel)]
    by_x, by_y, near = run_kernel(
        pack_kernel,
        [(2 * height, width)] * 2 + [(5 * height, width)],
        [*near, *refl_parts],
        (),
        0,
        72 * height * width,
    )
    far = swap(near[:height], "row", 6)
    by_x, by_y = swap(by_x, "row", 2), swap(by_y, "row", 4)
    (sides,) = run_kernel(
        sides_kernel,
        [(width, wide)],
        [near, matrix],
        (),
        6 * height * width * wide,
        4 * height * (width + wide),
    )
    sides = sides + swap(sides, "row", 1)
    panels = stack(left_panel, right_panel)
    across_own = swap(panels, "row", 1)
    last, across_own = lax.optimization_barrier((stack(by_x, by_y, far), across_own))
    own_at = ((0, 0), (0, 1))
    near_at = ((0, 2), (2, 0), (2, 1), (4, 0), (4, 1))
    last_at = ((6, 0), (2, 2), (6, 1), (4, 2), (6, 2))

    def across(places):
        return tuple((index + 1, kind) for index, kind in places)

    found = [(panels, own_at), (across_own, across(own_at))]
    for value, places in ((near, near_at), (last, last_at)):
        found += [(value, places), (swap(value, "row", 1), across(places))]
    return found, near, sides, by_x


def core_sum(value):
    core = lax.axis_index("row") % 2
    half = value.shape[0] // 2
    kept = lax.dynamic_slice_in_dim(value, core * half, half, 0)
    given = lax.dynamic_slice_in_dim(value, (1 - core) * half, half, 0)
    return kept + swap(given, "row", 1)


def chips_sum(total, rows):
    bit = 2
    while bit < rows:
        total = total + swap(total, "row", bit)
        bit *= 2
    core = lax.axis_index("row") % 2
    other = swap(total, "row", 1)
    first = jnp.where(core == 0, total, other)
    second = jnp.where(core == 0, other, total)
    return jnp.concatenate([first, second], axis=0)


def order_blocks(value, per, first):
    width = value.shape[1] // per
    bit = 1
    while bit < per:
        parts = [value[:, t * width : (t + 1) * width] for t in range(per)]
        moved = jnp.concatenate([parts[t ^ bit] for t in range(per)], axis=1)
        value = jnp.where((first // bit) % 2 == 1, moved, value)
        bit *= 2
    return value


def place_in_kernel(per):
    row, col = lax.axis_index("row"), lax.axis_index("col")
    return (row // per) ^ col, row % per


def at_end():
    col = lax.axis_index("col")
    return (col == 0) | (col == lax.axis_size("col") - 1)


def split_pieces(pieces, in_refs, high, low, height, share):
    for ref, places in zip(in_refs, pieces):
        for n, (index, kind) in enumerate(places):
            upper, lower = halves(ref[n * height : (n + 1) * height, :])
            rows = slice(index * height, (index + 1) * height)
            columns = slice(kind * share, (kind + 1) * share)
            high[rows, columns] = upper
            low[rows, columns] = lower


def block_of(factors, high, low, begin, wide):
    height = factors.shape[0] // 2
    rows = pl.ds(pl.multiple_of(begin, 16), wide)

    def one(a, b):
        return lax.dot_general(a, b, (ALONG, ((), ())), preferred_element_type=jnp.float32)

    both = one(factors, high[rows, :])
    return both[:height] + (both[height:] + one(factors[:height], low[rows, :]))


def send_kernel(pieces, per, share, *refs):
    count = len(pieces)
    in_refs, matrix, factors_ref = refs[:count], refs[count], refs[count + 1]
    outs, (high, low) = refs[count + 2 : -2], refs[-2:]
    height = matrix.shape[0]
    wide = per * height
    base, first = place_in_kernel(per)
    split_pieces(pieces, in_refs, high, low, height, share)
    panels = (high[:, : 2 * share], low[:, : 2 * share])
    refl = (high[:, 2 * share :], low[:, 2 * share :])
    mixed_pair = halves(pair_dot(refl, panels, DOWN))
    left_panel, right_panel = in_refs[0][:height, :], in_refs[0][height:, :]
    own_refl = (high[:height, 2 * share :], low[:height, 2 * share :])
    spread = pair_dot(own_refl, mixed_pair, OVER)
    turned = halves(jnp.concatenate([right_panel, -left_panel], axis=1))
    image = pair_dot(turned, mixed_pair, ALONG)
    for t in range(per):
        begin = pl.multiple_of((base * per + (t ^ first)) * height, 16)
        rows = pl.ds(begin, height)
        image = image + pair_dot(
            halves(matrix[:, t * height : (t + 1) * height]),
            (high[rows, 2 * share :], low[rows, 2 * share :]),
            OVER,
        )
    factors = jnp.concatenate(
        [right_panel - spread[:, share:], spread[:, :share] - left_panel, -image], axis=1
    )
    factors_ref[...] = factors
    stacked = jnp.concatenate(halves(factors), axis=0)
    onward = jnp.where(at_end(), 3, 1)
    for k, out in zip((onward, 2, 4 - onward), outs):
        out[...] = block_of(stacked, high, low, (base ^ k) * wide, wide)


def keep_kernel(pieces, per, share, *refs):
    count = len(pieces)
    in_refs, (factors_ref, matrix, out, high, low, made) = refs[:count], refs[count:]
    height = matrix.shape[0]
    wide = per * height
    base, first = place_in_kernel(per)
    split_pieces(pieces, in_refs, high, low, height, share)
    stacked = jnp.concatenate(halves(factors_ref[...]), axis=0)
    made[...] = block_of(stacked, high, low, base * wide, wide)
    put_in_order(out, matrix, made, first, per)


def put_in_order(out, base, total, first, per):
    height = out.shape[0]
    for other in range(per):

        @pl.when(first == other)
        def _():
            for t in range(per):
                here = slice(t * height, (t + 1) * height)
                there = slice((t ^ other) * height, ((t ^ other) + 1) * height)
                out[:, here] = base[:, here] + total[:, there]


def sides_kernel(near, matrix, out):
    refl = near[: matrix.shape[0], :]
    out[...] = pair_dot(halves(refl), halves(matrix[...]), DOWN)


def sum_kernel(per, *refs):
    *blocks, base, out, made = refs
    _, first = place_in_kernel(per)
    total = blocks[0][...]
    for block in blocks[1:]:
        total = total + block[...]
    made[...] = total
    put_in_order(out, base, made, first, per)


def late_kernel(passed, across, other, sides, beside, out, added):
    added[...] = sides[...] + beside[...]

    @pl.when(at_end())
    def _():
        out[...] = other[...]

    @pl.when(jnp.logical_not(at_end()))
    def _():
        out[...] = passed[...] + across[...]


def last_kernel(per, *refs):
    summed, late, passed, sides, *parts, near, out, made = refs
    _, first = place_in_kernel(per)
    made[...] = late[...]

    @pl.when(at_end())
    def _():
        made[...] = made[...] + passed[...]

    put_in_order(out, summed, made, first, per)
    refl = near[: out.shape[0], :]
    whole = sides[...] + jnp.concatenate([part[...] for part in parts], axis=0)
    out[...] = out[...] - pair_dot(halves(refl), halves(whole), OVER)


def run_kernel(body, outs, args, scratch=(), flops=0, moved=0):
    vmem = pl.BlockSpec(memory_space=pltpu.VMEM)
    return pl.pallas_call(
        body,
        out_shape=[jax.ShapeDtypeStruct(shape, jnp.float32) for shape in outs],
        in_specs=[vmem] * len(args),
        out_specs=[vmem] * len(outs),
        scratch_shapes=list(scratch),
        compiler_params=pltpu.CompilerParams(vmem_limit_bytes=VMEM_BYTES),
        cost_estimate=pl.CostEstimate(flops=flops, bytes_accessed=moved, transcendentals=0),
    )(*args)


def blocks_plain(panels, refls, matrix, base, first, cols, per):
    all_panels, all_refl = jnp.concatenate(panels, axis=0), jnp.concatenate(refls, axis=0)
    own, own_refl = panels[0], refls[0]
    height, share = own.shape[0], own.shape[1] // 2
    wide = per * height
    left_panel, right_panel = own[:, :share], own[:, share:]
    mixed = dot(all_panels, all_refl, DOWN)
    mixed_left, mixed_right = mixed[:share], mixed[share:]
    mine = order_blocks(matrix, per, first)
    col_refl = lax.dynamic_slice_in_dim(all_refl, base * wide, wide, 0)
    image = (
        dot(right_panel, mixed_left, OVER)
        - dot(left_panel, mixed_right, OVER)
        + dot(mine, col_refl, OVER)
    )
    factors = jnp.concatenate(
        [
            right_panel - dot(own_refl, mixed_right, ALONG),
            dot(own_refl, mixed_left, ALONG) - left_panel,
            -image,
        ],
        axis=1,
    )
    whole = jnp.concatenate([all_panels, all_refl], axis=1)
    return [
        dot(factors, lax.dynamic_slice_in_dim(whole, (base ^ k) * wide, wide, 0), ALONG)
        for k in range(cols)
    ]


def gather_columns(reflectors, cols):
    value, bit = reflectors, 1
    while bit < cols:
        value = jnp.concatenate([value, swap(value, "col", bit)], axis=1)
        bit *= 2
    return value


def local_square(matrix, left_panel, right_panel, reflectors):
    rows, cols = lax.axis_size("row"), lax.axis_size("col")
    per = rows // cols
    height, share = left_panel.shape
    wide = per * height
    refl_parts, bit = [reflectors.T], 1
    while bit < cols:
        known = jnp.concatenate(refl_parts, axis=0)
        refl_parts = [known, swap(known, "col", bit)]
        bit *= 2
    found, near, sides, by_x = gather_square(left_panel, right_panel, refl_parts, matrix)
    width = share
    sides, _ = lax.optimization_barrier((sides, by_x))
    beside = swap(sides, "row", 2)

    arrays = [value for value, _ in found]
    pieces = tuple(places for _, places in found)
    total, depth = rows * height, 2 * share + width
    halved = pltpu.VMEM((total, depth), jnp.bfloat16)
    block = pltpu.VMEM((height, wide), jnp.float32)
    factors, *blocks = run_kernel(
        functools.partial(send_kernel, pieces, per, share),
        [(height, depth)] + [(height, wide)] * (cols - 1),
        arrays + [matrix],
        [halved, halved],
        12 * total * share * width + 6 * total * height * depth,
        4 * total * depth,
    )
    received = [lax.ppermute(blocks[2], "col", [(1, 2), (2, 1)])]
    passed = swap(blocks[0], "col", 1)
    received += [lax.ppermute(blocks[1], "col", [(0, 2), (3, 1)])]
    late, sides = run_kernel(
        late_kernel,
        [(height, wide), (width, wide)],
        [passed, blocks[1], blocks[2], sides, beside],
    )
    late = lax.ppermute(late, "col", [(0, 1), (3, 2), (1, 3), (2, 0)])
    (base,) = run_kernel(
        functools.partial(keep_kernel, pieces, per, share),
        [(height, wide)],
        arrays + [factors, matrix],
        [halved, halved, block],
        6 * wide * height * depth,
        4 * total * depth,
    )
    parts = [swap(sides[n : n + width // 2], "row", 4) for n in (0, width // 2)]
    (summed,) = run_kernel(
        functools.partial(sum_kernel, per),
        [(height, wide)],
        [*received, base],
        [block],
        height * wide * cols,
        16 * height * wide * (cols + 1),
    )
    summed, parts, late = lax.optimization_barrier((summed, parts, late))
    (updated,) = run_kernel(
        functools.partial(last_kernel, per),
        [(height, wide)],
        [summed, late, passed, sides, *parts, near],
        [block],
        6 * height * width * wide,
        4 * width * wide * 2,
    )
    return updated


def local_general(matrix, left_panel, right_panel, reflectors):
    rows, cols = lax.axis_size("row"), lax.axis_size("col")
    per = rows // cols
    row, col = lax.axis_index("row"), lax.axis_index("col")
    base, first = (row // per) ^ col, row % per
    own_refl = gather_columns(reflectors, cols)
    panels = gather_row(jnp.concatenate([left_panel, right_panel], axis=1), rows)
    refls = gather_row(own_refl, rows)
    made = blocks_plain(panels, refls, matrix, base, first, cols, per)
    total = made[0]
    for k in range(1, cols):
        total = total + swap(made[k], "col", k)
    sides = chips_sum(core_sum(dot(own_refl, matrix, DOWN)), rows)
    return order_blocks(total, per, first) + (matrix - dot(own_refl, sides, OVER))


def local(matrix, left_panel, right_panel, reflectors):
    rows, cols = lax.axis_size("row"), lax.axis_size("col")
    height, share = left_panel.shape
    width = reflectors.shape[1] * cols
    need = rows * height * (2 * share + width) * 8 + rows * height * height * 8
    if rows == 8 and cols == 4 and share == width and need <= VMEM_BYTES:
        return local_square(matrix, left_panel, right_panel, reflectors)
    return local_general(matrix, left_panel, right_panel, reflectors)


def solution(mesh):
    spec = P("row", "col")
    return jax.shard_map(
        local, mesh=mesh, in_specs=(spec,) * 4, out_specs=spec, check_vma=False
    )
```

```python
import functools

import jax
import jax.numpy as jnp
from jax import lax
from jax.experimental import pallas as pl
from jax.experimental.pallas import tpu as pltpu
from jax.sharding import PartitionSpec as P

ALONG = ((1,), (1,))
OVER = ((1,), (0,))
DOWN = ((0,), (0,))
VMEM_BYTES = 24 * 2**20


def dot(first, second, dims):
    return lax.dot_general(
        first,
        second,
        (dims, ((), ())),
        precision=lax.Precision.HIGH,
        preferred_element_type=jnp.float32,
    )


def halves(value):
    high = value.astype(jnp.bfloat16)
    return high, (value - high.astype(jnp.float32)).astype(jnp.bfloat16)


def pair_dot(first, second, dims):
    def one(a, b):
        return lax.dot_general(a, b, (dims, ((), ())), preferred_element_type=jnp.float32)

    return one(first[0], second[0]) + (one(first[0], second[1]) + one(first[1], second[0]))


def swap(value, axis, offset):
    size = lax.axis_size(axis)
    return lax.ppermute(value, axis, [(i, i ^ offset) for i in range(size)])


def gather_row(value, rows):
    blocks = []
    for chip in range(0, rows, 2):
        here = swap(value, "row", chip) if chip else value
        blocks += [here, swap(here, "row", 1)]
    return blocks


def stack(*parts):
    return jnp.concatenate(parts, axis=0)


def pack_kernel(left_x, right_x, left_y, right_y, *refs):
    *parts, by_x, by_y, near = refs
    height = left_x.shape[0]
    near[:height, :] = jnp.concatenate([part[...] for part in parts], axis=0).T
    for n, value in enumerate((left_x, right_x, left_y, right_y)):
        near[(n + 1) * height : (n + 2) * height, :] = value[...]
    by_x[:height, :] = left_y[...]
    by_x[height:, :] = near[:height, :]
    by_y[:height, :] = right_x[...]
    by_y[height:, :] = near[:height, :]


def gather_square(left_panel, right_panel, refl_parts, matrix):
    height, width = left_panel.shape
    wide = matrix.shape[1]
    near = [swap(panel, "row", bits) for bits in (2, 4) for panel in (left_panel, right_panel)]
    by_x, by_y, near = run_kernel(
        pack_kernel,
        [(2 * height, width)] * 2 + [(5 * height, width)],
        [*near, *refl_parts],
        (),
        0,
        72 * height * width,
    )
    far = swap(near[:height], "row", 6)
    by_x, by_y = swap(by_x, "row", 2), swap(by_y, "row", 4)
    (sides,) = run_kernel(
        sides_kernel,
        [(width, wide)],
        [near, matrix],
        (),
        6 * height * width * wide,
        4 * height * (width + wide),
    )
    across_sides = swap(sides, "row", 1)
    panels = stack(left_panel, right_panel)
    across_own = swap(panels, "row", 1)
    last, across_own, _ = lax.optimization_barrier(
        (stack(by_x, by_y, far), across_own, across_sides)
    )
    sides = sides + across_sides
    own_at = ((0, 0), (0, 1))
    near_at = ((0, 2), (2, 0), (2, 1), (4, 0), (4, 1))
    last_at = ((6, 0), (2, 2), (6, 1), (4, 2), (6, 2))

    def across(places):
        return tuple((index + 1, kind) for index, kind in places)

    found = [(panels, own_at), (across_own, across(own_at))]
    for value, places in ((near, near_at), (last, last_at)):
        found += [(value, places), (swap(value, "row", 1), across(places))]
    return found, near, sides, by_x


def core_sum(value):
    core = lax.axis_index("row") % 2
    half = value.shape[0] // 2
    kept = lax.dynamic_slice_in_dim(value, core * half, half, 0)
    given = lax.dynamic_slice_in_dim(value, (1 - core) * half, half, 0)
    return kept + swap(given, "row", 1)


def chips_sum(total, rows):
    bit = 2
    while bit < rows:
        total = total + swap(total, "row", bit)
        bit *= 2
    core = lax.axis_index("row") % 2
    other = swap(total, "row", 1)
    first = jnp.where(core == 0, total, other)
    second = jnp.where(core == 0, other, total)
    return jnp.concatenate([first, second], axis=0)


def order_blocks(value, per, first):
    width = value.shape[1] // per
    bit = 1
    while bit < per:
        parts = [value[:, t * width : (t + 1) * width] for t in range(per)]
        moved = jnp.concatenate([parts[t ^ bit] for t in range(per)], axis=1)
        value = jnp.where((first // bit) % 2 == 1, moved, value)
        bit *= 2
    return value


def place_in_kernel(per):
    row, col = lax.axis_index("row"), lax.axis_index("col")
    return (row // per) ^ col, row % per


def at_end():
    col = lax.axis_index("col")
    return (col == 0) | (col == lax.axis_size("col") - 1)


def split_pieces(pieces, in_refs, high, low, height, share):
    for ref, places in zip(in_refs, pieces):
        for n, (index, kind) in enumerate(places):
            upper, lower = halves(ref[n * height : (n + 1) * height, :])
            rows = slice(index * height, (index + 1) * height)
            columns = slice(kind * share, (kind + 1) * share)
            high[rows, columns] = upper
            low[rows, columns] = lower


def block_of(factors, high, low, begin, wide):
    height = factors.shape[0] // 2
    rows = pl.ds(pl.multiple_of(begin, 16), wide)

    def one(a, b):
        return lax.dot_general(a, b, (ALONG, ((), ())), preferred_element_type=jnp.float32)

    both = one(factors, high[rows, :])
    return both[:height] + (both[height:] + one(factors[:height], low[rows, :]))


def of_core(matrix, first, same):
    height = matrix.shape[0]
    return jnp.where((first == 0) == same, matrix[:, :height], matrix[:, height:])


def mix_kernel(pieces, order, per, share, *refs):
    count = len(pieces)
    in_refs, (matrix, mixed, image, high, low) = refs[:count], refs[count:]
    height = matrix.shape[0]
    for ref, places in zip(in_refs, pieces):
        for n, (index, kind) in enumerate(places):
            upper, lower = halves(ref[n * height : (n + 1) * height, :])
            rows = slice(order.index(index) * height, (order.index(index) + 1) * height)
            columns = slice(kind * share, (kind + 1) * share)
            high[rows, columns] = upper
            low[rows, columns] = lower
    panels = (high[:, : 2 * share], low[:, : 2 * share])
    refl = (high[:, 2 * share :], low[:, 2 * share :])
    mixed[...] = pair_dot(refl, panels, DOWN)
    base, first = place_in_kernel(per)
    rows = pl.ds(pl.multiple_of(base * height, 16), height)
    image[...] = pair_dot(
        halves(of_core(matrix, first, True)), (high[rows, 2 * share :], low[rows, 2 * share :]), OVER
    )


def send_kernel(pieces, order, per, share, *refs):
    count = len(pieces)
    in_refs, (mixed_ref, image_ref, matrix, factors_ref) = refs[:count], refs[count : count + 4]
    outs, (high, low) = refs[count + 4 : -2], refs[-2:]
    height = matrix.shape[0]
    wide = per * height
    base, first = place_in_kernel(per)
    split_pieces(pieces, in_refs, high, low, height, share)
    mixed = mixed_ref[...]
    for index in range(high.shape[0] // height):
        if index not in order:
            rows = slice(index * height, (index + 1) * height)
            panels = (high[rows, : 2 * share], low[rows, : 2 * share])
            refl = (high[rows, 2 * share :], low[rows, 2 * share :])
            mixed = mixed + pair_dot(refl, panels, DOWN)
    mixed_pair = halves(mixed)
    left_panel, right_panel = in_refs[0][:height, :], in_refs[0][height:, :]
    own_refl = (high[:height, 2 * share :], low[:height, 2 * share :])
    rows = pl.ds(pl.multiple_of((base * per + 1) * height, 16), height)
    image = image_ref[...] + pair_dot(
        halves(of_core(matrix, first, False)),
        (high[rows, 2 * share :], low[rows, 2 * share :]),
        OVER,
    )
    spread = pair_dot(own_refl, mixed_pair, OVER)
    turned = halves(jnp.concatenate([right_panel, -left_panel], axis=1))
    image = image + pair_dot(turned, mixed_pair, ALONG)
    factors = jnp.concatenate(
        [right_panel - spread[:, share:], spread[:, :share] - left_panel, -image], axis=1
    )
    factors_ref[...] = factors
    stacked = jnp.concatenate(halves(factors), axis=0)
    onward = jnp.where(at_end(), 3, 1)
    for k, out in zip((onward, 2, 4 - onward), outs):
        out[...] = block_of(stacked, high, low, (base ^ k) * wide, wide)


def keep_kernel(pieces, per, share, *refs):
    count = len(pieces)
    in_refs, (factors_ref, matrix, out, high, low, made) = refs[:count], refs[count:]
    height = matrix.shape[0]
    wide = per * height
    base, first = place_in_kernel(per)
    split_pieces(pieces, in_refs, high, low, height, share)
    stacked = jnp.concatenate(halves(factors_ref[...]), axis=0)
    made[...] = block_of(stacked, high, low, base * wide, wide)
    put_in_order(out, matrix, made, first, per)


def put_in_order(out, base, total, first, per):
    height = out.shape[0]
    for other in range(per):

        @pl.when(first == other)
        def _():
            for t in range(per):
                here = slice(t * height, (t + 1) * height)
                there = slice((t ^ other) * height, ((t ^ other) + 1) * height)
                out[:, here] = base[:, here] + total[:, there]


def sides_kernel(near, matrix, out):
    refl = near[: matrix.shape[0], :]
    out[...] = pair_dot(halves(refl), halves(matrix[...]), DOWN)


def sum_kernel(per, *refs):
    *blocks, base, out, made = refs
    _, first = place_in_kernel(per)
    total = blocks[0][...]
    for block in blocks[1:]:
        total = total + block[...]
    made[...] = total
    put_in_order(out, base, made, first, per)


def late_kernel(passed, across, other, sides, beside, out, added):
    added[...] = sides[...] + beside[...]

    @pl.when(at_end())
    def _():
        out[...] = other[...]

    @pl.when(jnp.logical_not(at_end()))
    def _():
        out[...] = passed[...] + across[...]


def last_kernel(per, *refs):
    summed, late, passed, sides, *parts, near, out, made = refs
    _, first = place_in_kernel(per)
    made[...] = late[...]

    @pl.when(at_end())
    def _():
        made[...] = made[...] + passed[...]

    put_in_order(out, summed, made, first, per)
    refl = near[: out.shape[0], :]
    whole = sides[...] + jnp.concatenate([part[...] for part in parts], axis=0)
    out[...] = out[...] - pair_dot(halves(refl), halves(whole), OVER)


def run_kernel(body, outs, args, scratch=(), flops=0, moved=0):
    vmem = pl.BlockSpec(memory_space=pltpu.VMEM)
    return pl.pallas_call(
        body,
        out_shape=[jax.ShapeDtypeStruct(shape, jnp.float32) for shape in outs],
        in_specs=[vmem] * len(args),
        out_specs=[vmem] * len(outs),
        scratch_shapes=list(scratch),
        compiler_params=pltpu.CompilerParams(vmem_limit_bytes=VMEM_BYTES),
        cost_estimate=pl.CostEstimate(flops=flops, bytes_accessed=moved, transcendentals=0),
    )(*args)


def blocks_plain(panels, refls, matrix, base, first, cols, per):
    all_panels, all_refl = jnp.concatenate(panels, axis=0), jnp.concatenate(refls, axis=0)
    own, own_refl = panels[0], refls[0]
    height, share = own.shape[0], own.shape[1] // 2
    wide = per * height
    left_panel, right_panel = own[:, :share], own[:, share:]
    mixed = dot(all_panels, all_refl, DOWN)
    mixed_left, mixed_right = mixed[:share], mixed[share:]
    mine = order_blocks(matrix, per, first)
    col_refl = lax.dynamic_slice_in_dim(all_refl, base * wide, wide, 0)
    image = (
        dot(right_panel, mixed_left, OVER)
        - dot(left_panel, mixed_right, OVER)
        + dot(mine, col_refl, OVER)
    )
    factors = jnp.concatenate(
        [
            right_panel - dot(own_refl, mixed_right, ALONG),
            dot(own_refl, mixed_left, ALONG) - left_panel,
            -image,
        ],
        axis=1,
    )
    whole = jnp.concatenate([all_panels, all_refl], axis=1)
    return [
        dot(factors, lax.dynamic_slice_in_dim(whole, (base ^ k) * wide, wide, 0), ALONG)
        for k in range(cols)
    ]


def gather_columns(reflectors, cols):
    value, bit = reflectors, 1
    while bit < cols:
        value = jnp.concatenate([value, swap(value, "col", bit)], axis=1)
        bit *= 2
    return value


def local_square(matrix, left_panel, right_panel, reflectors):
    rows, cols = lax.axis_size("row"), lax.axis_size("col")
    per = rows // cols
    height, share = left_panel.shape
    wide = per * height
    refl_parts, bit = [reflectors.T], 1
    while bit < cols:
        known = jnp.concatenate(refl_parts, axis=0)
        refl_parts = [known, swap(known, "col", bit)]
        bit *= 2
    found, near, sides, by_x = gather_square(left_panel, right_panel, refl_parts, matrix)
    width = share
    sides, _ = lax.optimization_barrier((sides, by_x))
    beside = swap(sides, "row", 2)

    arrays = [value for value, _ in found]
    pieces = tuple(places for _, places in found)
    total, depth = rows * height, 2 * share + width
    halved = pltpu.VMEM((total, depth), jnp.bfloat16)
    block = pltpu.VMEM((height, wide), jnp.float32)
    order = tuple(range(0, rows, 2))
    mine = [n for n, places in enumerate(pieces) if all(i in order for i, _ in places)]
    known = pltpu.VMEM((len(order) * height, depth), jnp.bfloat16)
    mixed, image = run_kernel(
        functools.partial(mix_kernel, tuple(pieces[n] for n in mine), order, per, share),
        [(width, 2 * share), (height, width)],
        [arrays[n] for n in mine] + [matrix],
        [known, known],
        12 * len(order) * height * share * width,
        4 * len(order) * height * depth,
    )
    factors, *blocks = run_kernel(
        functools.partial(send_kernel, pieces, order, per, share),
        [(height, depth)] + [(height, wide)] * (cols - 1),
        arrays + [mixed, image, matrix],
        [halved, halved],
        12 * (total - len(order) * height) * share * width + 6 * total * height * depth,
        4 * total * depth,
    )
    received = [lax.ppermute(blocks[2], "col", [(1, 2), (2, 1)])]
    passed = swap(blocks[0], "col", 1)
    received += [lax.ppermute(blocks[1], "col", [(0, 2), (3, 1)])]
    late, sides = run_kernel(
        late_kernel,
        [(height, wide), (width, wide)],
        [passed, blocks[1], blocks[2], sides, beside],
    )
    late = lax.ppermute(late, "col", [(0, 1), (3, 2), (1, 3), (2, 0)])
    (base,) = run_kernel(
        functools.partial(keep_kernel, pieces, per, share),
        [(height, wide)],
        arrays + [factors, matrix],
        [halved, halved, block],
        6 * wide * height * depth,
        4 * total * depth,
    )
    parts = [swap(sides[n : n + width // 2], "row", 4) for n in (0, width // 2)]
    (summed,) = run_kernel(
        functools.partial(sum_kernel, per),
        [(height, wide)],
        [*received, base],
        [block],
        height * wide * cols,
        16 * height * wide * (cols + 1),
    )
    summed, parts, late = lax.optimization_barrier((summed, parts, late))
    (updated,) = run_kernel(
        functools.partial(last_kernel, per),
        [(height, wide)],
        [summed, late, passed, sides, *parts, near],
        [block],
        6 * height * width * wide,
        4 * width * wide * 2,
    )
    return updated


def local_general(matrix, left_panel, right_panel, reflectors):
    rows, cols = lax.axis_size("row"), lax.axis_size("col")
    per = rows // cols
    row, col = lax.axis_index("row"), lax.axis_index("col")
    base, first = (row // per) ^ col, row % per
    own_refl = gather_columns(reflectors, cols)
    panels = gather_row(jnp.concatenate([left_panel, right_panel], axis=1), rows)
    refls = gather_row(own_refl, rows)
    made = blocks_plain(panels, refls, matrix, base, first, cols, per)
    total = made[0]
    for k in range(1, cols):
        total = total + swap(made[k], "col", k)
    sides = chips_sum(core_sum(dot(own_refl, matrix, DOWN)), rows)
    return order_blocks(total, per, first) + (matrix - dot(own_refl, sides, OVER))


def local(matrix, left_panel, right_panel, reflectors):
    rows, cols = lax.axis_size("row"), lax.axis_size("col")
    height, share = left_panel.shape
    width = reflectors.shape[1] * cols
    need = rows * height * (2 * share + width) * 8 + rows * height * height * 8
    if rows == 8 and cols == 4 and share == width and need <= VMEM_BYTES:
        return local_square(matrix, left_panel, right_panel, reflectors)
    return local_general(matrix, left_panel, right_panel, reflectors)


def solution(mesh):
    spec = P("row", "col")
    return jax.shard_map(
        local, mesh=mesh, in_specs=(spec,) * 4, out_specs=spec, check_vma=False
    )
```

```python
import functools

import jax
import jax.numpy as jnp
from jax import lax
from jax.experimental import pallas as pl
from jax.experimental.pallas import tpu as pltpu
from jax.sharding import PartitionSpec as P

ALONG = ((1,), (1,))
OVER = ((1,), (0,))
DOWN = ((0,), (0,))
VMEM_BYTES = 24 * 2**20


def dot(first, second, dims):
    return lax.dot_general(
        first,
        second,
        (dims, ((), ())),
        precision=lax.Precision.HIGH,
        preferred_element_type=jnp.float32,
    )


def halves(value):
    high = value.astype(jnp.bfloat16)
    return high, (value - high.astype(jnp.float32)).astype(jnp.bfloat16)


def pair_dot(first, second, dims):
    def one(a, b):
        return lax.dot_general(a, b, (dims, ((), ())), preferred_element_type=jnp.float32)

    return one(first[0], second[0]) + (one(first[0], second[1]) + one(first[1], second[0]))


def swap(value, axis, offset):
    size = lax.axis_size(axis)
    return lax.ppermute(value, axis, [(i, i ^ offset) for i in range(size)])


def gather_row(value, rows):
    blocks = []
    for chip in range(0, rows, 2):
        here = swap(value, "row", chip) if chip else value
        blocks += [here, swap(here, "row", 1)]
    return blocks


def stack(*parts):
    return jnp.concatenate(parts, axis=0)


def pack_kernel(left_x, right_x, left_y, right_y, *refs):
    *parts, by_x, by_y, near = refs
    height = left_x.shape[0]
    near[:height, :] = jnp.concatenate([part[...] for part in parts], axis=0).T
    for n, value in enumerate((left_x, right_x, left_y, right_y)):
        near[(n + 1) * height : (n + 2) * height, :] = value[...]
    by_x[:height, :] = left_y[...]
    by_x[height:, :] = near[:height, :]
    by_y[:height, :] = right_x[...]
    by_y[height:, :] = near[:height, :]


def gather_square(left_panel, right_panel, refl_parts, matrix):
    height, width = left_panel.shape
    wide = matrix.shape[1]
    near = [swap(panel, "row", bits) for bits in (2, 4) for panel in (left_panel, right_panel)]
    by_x, by_y, near = run_kernel(
        pack_kernel,
        [(2 * height, width)] * 2 + [(5 * height, width)],
        [*near, *refl_parts],
        (),
        0,
        72 * height * width,
    )
    far = swap(near[:height], "row", 6)
    by_x, by_y = swap(by_x, "row", 2), swap(by_y, "row", 4)
    (sides,) = run_kernel(
        sides_kernel,
        [(width, wide)],
        [near, matrix],
        (),
        6 * height * width * wide,
        4 * height * (width + wide),
    )
    across_sides = swap(sides, "row", 1)
    panels = stack(left_panel, right_panel)
    across_own = swap(panels, "row", 1)
    last, across_own, _ = lax.optimization_barrier(
        (stack(by_x, by_y, far), across_own, across_sides)
    )
    sides = sides + across_sides
    own_at = ((0, 0), (0, 1))
    near_at = ((0, 2), (2, 0), (2, 1), (4, 0), (4, 1))
    last_at = ((6, 0), (2, 2), (6, 1), (4, 2), (6, 2))

    def across(places):
        return tuple((index + 1, kind) for index, kind in places)

    found = [(panels, own_at), (across_own, across(own_at))]
    for value, places in ((near, near_at), (last, last_at)):
        found += [(value, places), (swap(value, "row", 1), across(places))]
    return found, near, sides, by_x


def core_sum(value):
    core = lax.axis_index("row") % 2
    half = value.shape[0] // 2
    kept = lax.dynamic_slice_in_dim(value, core * half, half, 0)
    given = lax.dynamic_slice_in_dim(value, (1 - core) * half, half, 0)
    return kept + swap(given, "row", 1)


def chips_sum(total, rows):
    bit = 2
    while bit < rows:
        total = total + swap(total, "row", bit)
        bit *= 2
    core = lax.axis_index("row") % 2
    other = swap(total, "row", 1)
    first = jnp.where(core == 0, total, other)
    second = jnp.where(core == 0, other, total)
    return jnp.concatenate([first, second], axis=0)


def order_blocks(value, per, first):
    width = value.shape[1] // per
    bit = 1
    while bit < per:
        parts = [value[:, t * width : (t + 1) * width] for t in range(per)]
        moved = jnp.concatenate([parts[t ^ bit] for t in range(per)], axis=1)
        value = jnp.where((first // bit) % 2 == 1, moved, value)
        bit *= 2
    return value


def place_in_kernel(per):
    row, col = lax.axis_index("row"), lax.axis_index("col")
    return (row // per) ^ col, row % per


def at_end():
    col = lax.axis_index("col")
    return (col == 0) | (col == lax.axis_size("col") - 1)


def split_pieces(pieces, in_refs, high, low, height, share):
    for ref, places in zip(in_refs, pieces):
        for n, (index, kind) in enumerate(places):
            upper, lower = halves(ref[n * height : (n + 1) * height, :])
            rows = slice(index * height, (index + 1) * height)
            columns = slice(kind * share, (kind + 1) * share)
            high[rows, columns] = upper
            low[rows, columns] = lower


def block_of(factors, high, low, begin, wide):
    height = factors.shape[0] // 2
    rows = pl.ds(pl.multiple_of(begin, 16), wide)

    def one(a, b):
        return lax.dot_general(a, b, (ALONG, ((), ())), preferred_element_type=jnp.float32)

    both = one(factors, high[rows, :])
    return both[:height] + (both[height:] + one(factors[:height], low[rows, :]))


def of_core(matrix, first, same):
    height = matrix.shape[0]
    return jnp.where((first == 0) == same, matrix[:, :height], matrix[:, height:])


def mix_kernel(pieces, order, per, share, *refs):
    count = len(pieces)
    in_refs, (matrix, mixed, image, high, low) = refs[:count], refs[count:]
    height = matrix.shape[0]
    for ref, places in zip(in_refs, pieces):
        for n, (index, kind) in enumerate(places):
            upper, lower = halves(ref[n * height : (n + 1) * height, :])
            rows = slice(order.index(index) * height, (order.index(index) + 1) * height)
            columns = slice(kind * share, (kind + 1) * share)
            high[rows, columns] = upper
            low[rows, columns] = lower
    panels = (high[:, : 2 * share], low[:, : 2 * share])
    refl = (high[:, 2 * share :], low[:, 2 * share :])
    mixed[...] = pair_dot(refl, panels, DOWN)
    base, first = place_in_kernel(per)
    rows = pl.ds(pl.multiple_of(base * height, 16), height)
    image[...] = pair_dot(
        halves(of_core(matrix, first, True)), (high[rows, 2 * share :], low[rows, 2 * share :]), OVER
    )


def send_kernel(pieces, order, per, share, *refs):
    count = len(pieces)
    in_refs, (mixed_ref, image_ref, matrix, factors_ref) = refs[:count], refs[count : count + 4]
    outs, (high, low) = refs[count + 4 : -2], refs[-2:]
    height = matrix.shape[0]
    wide = per * height
    base, first = place_in_kernel(per)
    split_pieces(pieces, in_refs, high, low, height, share)
    mixed = mixed_ref[...]
    for index in range(high.shape[0] // height):
        if index not in order:
            rows = slice(index * height, (index + 1) * height)
            panels = (high[rows, : 2 * share], low[rows, : 2 * share])
            refl = (high[rows, 2 * share :], low[rows, 2 * share :])
            mixed = mixed + pair_dot(refl, panels, DOWN)
    mixed_pair = halves(mixed)
    left_panel, right_panel = in_refs[0][:height, :], in_refs[0][height:, :]
    own_refl = (high[:height, 2 * share :], low[:height, 2 * share :])
    rows = pl.ds(pl.multiple_of((base * per + 1) * height, 16), height)
    image = image_ref[...] + pair_dot(
        halves(of_core(matrix, first, False)),
        (high[rows, 2 * share :], low[rows, 2 * share :]),
        OVER,
    )
    spread = pair_dot(own_refl, mixed_pair, OVER)
    turned = halves(jnp.concatenate([right_panel, -left_panel], axis=1))
    image = image + pair_dot(turned, mixed_pair, ALONG)
    factors = jnp.concatenate(
        [right_panel - spread[:, share:], spread[:, :share] - left_panel, -image], axis=1
    )
    factors_ref[...] = factors
    stacked = jnp.concatenate(halves(factors), axis=0)
    onward = jnp.where(at_end(), 3, 1)
    for k, out in zip((onward, 2, 4 - onward), outs):
        out[...] = block_of(stacked, high, low, (base ^ k) * wide, wide)


def keep_kernel(pieces, per, share, *refs):
    count = len(pieces)
    in_refs, (factors_ref, matrix, out, high, low, made) = refs[:count], refs[count:]
    height = matrix.shape[0]
    wide = per * height
    base, first = place_in_kernel(per)
    split_pieces(pieces, in_refs, high, low, height, share)
    stacked = jnp.concatenate(halves(factors_ref[...]), axis=0)
    made[...] = block_of(stacked, high, low, base * wide, wide)
    put_in_order(out, matrix, made, first, per)


def put_in_order(out, base, total, first, per):
    height = out.shape[0]
    for other in range(per):

        @pl.when(first == other)
        def _():
            for t in range(per):
                here = slice(t * height, (t + 1) * height)
                there = slice((t ^ other) * height, ((t ^ other) + 1) * height)
                out[:, here] = base[:, here] + total[:, there]


def sides_kernel(near, matrix, out):
    refl = near[: matrix.shape[0], :]
    out[...] = pair_dot(halves(refl), halves(matrix[...]), DOWN)


def sum_kernel(per, *refs):
    *blocks, base, out, made = refs
    _, first = place_in_kernel(per)
    total = blocks[0][...]
    for block in blocks[1:]:
        total = total + block[...]
    made[...] = total
    put_in_order(out, base, made, first, per)


def late_kernel(passed, across, other, sides, beside, out, added):
    added[...] = sides[...] + beside[...]

    @pl.when(at_end())
    def _():
        out[...] = other[...]

    @pl.when(jnp.logical_not(at_end()))
    def _():
        out[...] = passed[...] + across[...]


def image_kernel(summed, sides, *refs):
    *parts, near, out = refs
    refl = near[: out.shape[0], :]
    whole = sides[...] + jnp.concatenate([part[...] for part in parts], axis=0)
    out[...] = summed[...] - pair_dot(halves(refl), halves(whole), OVER)


def last_kernel(per, summed, late, passed, out, made):
    _, first = place_in_kernel(per)
    made[...] = late[...]

    @pl.when(at_end())
    def _():
        made[...] = made[...] + passed[...]

    put_in_order(out, summed, made, first, per)


def run_kernel(body, outs, args, scratch=(), flops=0, moved=0):
    vmem = pl.BlockSpec(memory_space=pltpu.VMEM)
    return pl.pallas_call(
        body,
        out_shape=[jax.ShapeDtypeStruct(shape, jnp.float32) for shape in outs],
        in_specs=[vmem] * len(args),
        out_specs=[vmem] * len(outs),
        scratch_shapes=list(scratch),
        compiler_params=pltpu.CompilerParams(vmem_limit_bytes=VMEM_BYTES),
        cost_estimate=pl.CostEstimate(flops=flops, bytes_accessed=moved, transcendentals=0),
    )(*args)


def blocks_plain(panels, refls, matrix, base, first, cols, per):
    all_panels, all_refl = jnp.concatenate(panels, axis=0), jnp.concatenate(refls, axis=0)
    own, own_refl = panels[0], refls[0]
    height, share = own.shape[0], own.shape[1] // 2
    wide = per * height
    left_panel, right_panel = own[:, :share], own[:, share:]
    mixed = dot(all_panels, all_refl, DOWN)
    mixed_left, mixed_right = mixed[:share], mixed[share:]
    mine = order_blocks(matrix, per, first)
    col_refl = lax.dynamic_slice_in_dim(all_refl, base * wide, wide, 0)
    image = (
        dot(right_panel, mixed_left, OVER)
        - dot(left_panel, mixed_right, OVER)
        + dot(mine, col_refl, OVER)
    )
    factors = jnp.concatenate(
        [
            right_panel - dot(own_refl, mixed_right, ALONG),
            dot(own_refl, mixed_left, ALONG) - left_panel,
            -image,
        ],
        axis=1,
    )
    whole = jnp.concatenate([all_panels, all_refl], axis=1)
    return [
        dot(factors, lax.dynamic_slice_in_dim(whole, (base ^ k) * wide, wide, 0), ALONG)
        for k in range(cols)
    ]


def gather_columns(reflectors, cols):
    value, bit = reflectors, 1
    while bit < cols:
        value = jnp.concatenate([value, swap(value, "col", bit)], axis=1)
        bit *= 2
    return value


def local_square(matrix, left_panel, right_panel, reflectors):
    rows, cols = lax.axis_size("row"), lax.axis_size("col")
    per = rows // cols
    height, share = left_panel.shape
    wide = per * height
    refl_parts, bit = [reflectors.T], 1
    while bit < cols:
        known = jnp.concatenate(refl_parts, axis=0)
        refl_parts = [known, swap(known, "col", bit)]
        bit *= 2
    found, near, sides, by_x = gather_square(left_panel, right_panel, refl_parts, matrix)
    width = share
    sides, _ = lax.optimization_barrier((sides, by_x))
    beside = swap(sides, "row", 2)

    arrays = [value for value, _ in found]
    pieces = tuple(places for _, places in found)
    total, depth = rows * height, 2 * share + width
    halved = pltpu.VMEM((total, depth), jnp.bfloat16)
    block = pltpu.VMEM((height, wide), jnp.float32)
    order = tuple(range(0, rows, 2))
    mine = [n for n, places in enumerate(pieces) if all(i in order for i, _ in places)]
    known = pltpu.VMEM((len(order) * height, depth), jnp.bfloat16)
    mixed, image = run_kernel(
        functools.partial(mix_kernel, tuple(pieces[n] for n in mine), order, per, share),
        [(width, 2 * share), (height, width)],
        [arrays[n] for n in mine] + [matrix],
        [known, known],
        12 * len(order) * height * share * width,
        4 * len(order) * height * depth,
    )
    factors, *blocks = run_kernel(
        functools.partial(send_kernel, pieces, order, per, share),
        [(height, depth)] + [(height, wide)] * (cols - 1),
        arrays + [mixed, image, matrix],
        [halved, halved],
        12 * (total - len(order) * height) * share * width + 6 * total * height * depth,
        4 * total * depth,
    )
    received = [lax.ppermute(blocks[2], "col", [(1, 2), (2, 1)])]
    passed = swap(blocks[0], "col", 1)
    received += [lax.ppermute(blocks[1], "col", [(0, 2), (3, 1)])]
    late, sides = run_kernel(
        late_kernel,
        [(height, wide), (width, wide)],
        [passed, blocks[1], blocks[2], sides, beside],
    )
    late = lax.ppermute(late, "col", [(0, 1), (3, 2), (1, 3), (2, 0)])
    (base,) = run_kernel(
        functools.partial(keep_kernel, pieces, per, share),
        [(height, wide)],
        arrays + [factors, matrix],
        [halved, halved, block],
        6 * wide * height * depth,
        4 * total * depth,
    )
    parts = [swap(sides[n : n + width // 2], "row", 4) for n in (0, width // 2)]
    (summed,) = run_kernel(
        functools.partial(sum_kernel, per),
        [(height, wide)],
        [*received, base],
        [block],
        height * wide * cols,
        16 * height * wide * (cols + 1),
    )
    summed, parts = lax.optimization_barrier((summed, parts))
    (summed,) = run_kernel(
        image_kernel,
        [(height, wide)],
        [summed, sides, *parts, near],
        (),
        6 * height * width * wide,
        4 * width * wide * 2,
    )
    (updated,) = run_kernel(
        functools.partial(last_kernel, per),
        [(height, wide)],
        [summed, late, passed],
        [block],
        2 * height * wide,
        16 * height * wide,
    )
    return updated


def local_general(matrix, left_panel, right_panel, reflectors):
    rows, cols = lax.axis_size("row"), lax.axis_size("col")
    per = rows // cols
    row, col = lax.axis_index("row"), lax.axis_index("col")
    base, first = (row // per) ^ col, row % per
    own_refl = gather_columns(reflectors, cols)
    panels = gather_row(jnp.concatenate([left_panel, right_panel], axis=1), rows)
    refls = gather_row(own_refl, rows)
    made = blocks_plain(panels, refls, matrix, base, first, cols, per)
    total = made[0]
    for k in range(1, cols):
        total = total + swap(made[k], "col", k)
    sides = chips_sum(core_sum(dot(own_refl, matrix, DOWN)), rows)
    return order_blocks(total, per, first) + (matrix - dot(own_refl, sides, OVER))


def local(matrix, left_panel, right_panel, reflectors):
    rows, cols = lax.axis_size("row"), lax.axis_size("col")
    height, share = left_panel.shape
    width = reflectors.shape[1] * cols
    need = rows * height * (2 * share + width) * 8 + rows * height * height * 8
    if rows == 8 and cols == 4 and share == width and need <= VMEM_BYTES:
        return local_square(matrix, left_panel, right_panel, reflectors)
    return local_general(matrix, left_panel, right_panel, reflectors)


def solution(mesh):
    spec = P("row", "col")
    return jax.shard_map(
        local, mesh=mesh, in_specs=(spec,) * 4, out_specs=spec, check_vma=False
    )
```

```python
import functools

import jax
import jax.numpy as jnp
from jax import lax
from jax.experimental import pallas as pl
from jax.experimental.pallas import tpu as pltpu
from jax.sharding import PartitionSpec as P

ALONG = ((1,), (1,))
OVER = ((1,), (0,))
DOWN = ((0,), (0,))
VMEM_BYTES = 24 * 2**20


def dot(first, second, dims):
    return lax.dot_general(
        first,
        second,
        (dims, ((), ())),
        precision=lax.Precision.HIGH,
        preferred_element_type=jnp.float32,
    )


def halves(value):
    high = value.astype(jnp.bfloat16)
    return high, (value - high.astype(jnp.float32)).astype(jnp.bfloat16)


def pair_dot(first, second, dims):
    def one(a, b):
        return lax.dot_general(a, b, (dims, ((), ())), preferred_element_type=jnp.float32)

    return one(first[0], second[0]) + (one(first[0], second[1]) + one(first[1], second[0]))


def swap(value, axis, offset):
    size = lax.axis_size(axis)
    return lax.ppermute(value, axis, [(i, i ^ offset) for i in range(size)])


def gather_row(value, rows):
    blocks = []
    for chip in range(0, rows, 2):
        here = swap(value, "row", chip) if chip else value
        blocks += [here, swap(here, "row", 1)]
    return blocks


def stack(*parts):
    return jnp.concatenate(parts, axis=0)


def pack_kernel(left_x, right_x, left_y, right_y, *refs):
    *parts, by_x, by_y, near = refs
    height = left_x.shape[0]
    near[:height, :] = jnp.concatenate([part[...] for part in parts], axis=0).T
    for n, value in enumerate((left_x, right_x, left_y, right_y)):
        near[(n + 1) * height : (n + 2) * height, :] = value[...]
    by_x[:height, :] = left_y[...]
    by_x[height:, :] = near[:height, :]
    by_y[:height, :] = right_x[...]
    by_y[height:, :] = near[:height, :]


def gather_square(left_panel, right_panel, refl_parts, matrix):
    height, width = left_panel.shape
    wide = matrix.shape[1]
    near = [swap(panel, "row", bits) for bits in (2, 4) for panel in (left_panel, right_panel)]
    by_x, by_y, near = run_kernel(
        pack_kernel,
        [(2 * height, width)] * 2 + [(5 * height, width)],
        [*near, *refl_parts],
        (),
        0,
        72 * height * width,
    )
    far = swap(near[:height], "row", 6)
    by_x, by_y = swap(by_x, "row", 2), swap(by_y, "row", 4)
    (sides,) = run_kernel(
        sides_kernel,
        [(width, wide)],
        [near, matrix],
        (),
        6 * height * width * wide,
        4 * height * (width + wide),
    )
    across_sides = swap(sides, "row", 1)
    panels = stack(left_panel, right_panel)
    across_own = swap(panels, "row", 1)
    last, across_own, _ = lax.optimization_barrier(
        (stack(by_x, by_y, far), across_own, across_sides)
    )
    sides = sides + across_sides
    own_at = ((0, 0), (0, 1))
    near_at = ((0, 2), (2, 0), (2, 1), (4, 0), (4, 1))
    last_at = ((6, 0), (2, 2), (6, 1), (4, 2), (6, 2))

    def across(places):
        return tuple((index + 1, kind) for index, kind in places)

    found = [(panels, own_at), (across_own, across(own_at))]
    for value, places in ((near, near_at), (last, last_at)):
        found += [(value, places), (swap(value, "row", 1), across(places))]
    return found, near, sides, by_x


def core_sum(value):
    core = lax.axis_index("row") % 2
    half = value.shape[0] // 2
    kept = lax.dynamic_slice_in_dim(value, core * half, half, 0)
    given = lax.dynamic_slice_in_dim(value, (1 - core) * half, half, 0)
    return kept + swap(given, "row", 1)


def chips_sum(total, rows):
    bit = 2
    while bit < rows:
        total = total + swap(total, "row", bit)
        bit *= 2
    core = lax.axis_index("row") % 2
    other = swap(total, "row", 1)
    first = jnp.where(core == 0, total, other)
    second = jnp.where(core == 0, other, total)
    return jnp.concatenate([first, second], axis=0)


def order_blocks(value, per, first):
    width = value.shape[1] // per
    bit = 1
    while bit < per:
        parts = [value[:, t * width : (t + 1) * width] for t in range(per)]
        moved = jnp.concatenate([parts[t ^ bit] for t in range(per)], axis=1)
        value = jnp.where((first // bit) % 2 == 1, moved, value)
        bit *= 2
    return value


def place_in_kernel(per):
    row, col = lax.axis_index("row"), lax.axis_index("col")
    return (row // per) ^ col, row % per


def at_end():
    col = lax.axis_index("col")
    return (col == 0) | (col == lax.axis_size("col") - 1)


def split_pieces(pieces, in_refs, high, low, height, share):
    for ref, places in zip(in_refs, pieces):
        for n, (index, kind) in enumerate(places):
            upper, lower = halves(ref[n * height : (n + 1) * height, :])
            rows = slice(index * height, (index + 1) * height)
            columns = slice(kind * share, (kind + 1) * share)
            high[rows, columns] = upper
            low[rows, columns] = lower


def block_of(factors, high, low, begin, wide):
    height = factors.shape[0] // 2
    rows = pl.ds(pl.multiple_of(begin, 16), wide)

    def one(a, b):
        return lax.dot_general(a, b, (ALONG, ((), ())), preferred_element_type=jnp.float32)

    both = one(factors, high[rows, :])
    return both[:height] + (both[height:] + one(factors[:height], low[rows, :]))


def of_core(matrix, first, same):
    height = matrix.shape[0]
    return jnp.where((first == 0) == same, matrix[:, :height], matrix[:, height:])


def mix_kernel(pieces, order, per, share, *refs):
    count = len(pieces)
    in_refs, (matrix, mixed, image, high, low) = refs[:count], refs[count:]
    height = matrix.shape[0]
    for ref, places in zip(in_refs, pieces):
        for n, (index, kind) in enumerate(places):
            upper, lower = halves(ref[n * height : (n + 1) * height, :])
            rows = slice(order.index(index) * height, (order.index(index) + 1) * height)
            columns = slice(kind * share, (kind + 1) * share)
            high[rows, columns] = upper
            low[rows, columns] = lower
    panels = (high[:, : 2 * share], low[:, : 2 * share])
    refl = (high[:, 2 * share :], low[:, 2 * share :])
    mixed[...] = pair_dot(refl, panels, DOWN)
    base, first = place_in_kernel(per)
    rows = pl.ds(pl.multiple_of(base * height, 16), height)
    image[...] = pair_dot(
        halves(of_core(matrix, first, True)), (high[rows, 2 * share :], low[rows, 2 * share :]), OVER
    )


def send_kernel(pieces, order, per, share, *refs):
    count = len(pieces)
    in_refs, (mixed_ref, image_ref, matrix, factors_ref) = refs[:count], refs[count : count + 4]
    outs, (high, low) = refs[count + 4 : -2], refs[-2:]
    height = matrix.shape[0]
    wide = per * height
    base, first = place_in_kernel(per)
    split_pieces(pieces, in_refs, high, low, height, share)
    others = [index for index in range(high.shape[0] // height) if index not in order]

    def of_others(ref, columns):
        return jnp.concatenate(
            [ref[index * height : (index + 1) * height, columns] for index in others], axis=0
        )

    refl_at, panels_at = slice(2 * share, None), slice(0, 2 * share)
    mixed = mixed_ref[...] + pair_dot(
        (of_others(high, refl_at), of_others(low, refl_at)),
        (of_others(high, panels_at), of_others(low, panels_at)),
        DOWN,
    )
    mixed_pair = halves(mixed)
    left_panel, right_panel = in_refs[0][:height, :], in_refs[0][height:, :]
    own_refl = (high[:height, 2 * share :], low[:height, 2 * share :])
    rows = pl.ds(pl.multiple_of((base * per + 1) * height, 16), height)
    image = image_ref[...] + pair_dot(
        halves(of_core(matrix, first, False)),
        (high[rows, 2 * share :], low[rows, 2 * share :]),
        OVER,
    )
    spread = pair_dot(own_refl, mixed_pair, OVER)
    turned = halves(jnp.concatenate([right_panel, -left_panel], axis=1))
    image = image + pair_dot(turned, mixed_pair, ALONG)
    factors = jnp.concatenate(
        [right_panel - spread[:, share:], spread[:, :share] - left_panel, -image], axis=1
    )
    factors_ref[...] = factors
    stacked = jnp.concatenate(halves(factors), axis=0)
    onward = jnp.where(at_end(), 3, 1)
    for k, out in zip((onward, 2, 4 - onward), outs):
        out[...] = block_of(stacked, high, low, (base ^ k) * wide, wide)


def keep_kernel(pieces, per, share, *refs):
    count = len(pieces)
    in_refs, (factors_ref, matrix, out, high, low, made) = refs[:count], refs[count:]
    height = matrix.shape[0]
    wide = per * height
    base, first = place_in_kernel(per)
    split_pieces(pieces, in_refs, high, low, height, share)
    stacked = jnp.concatenate(halves(factors_ref[...]), axis=0)
    made[...] = block_of(stacked, high, low, base * wide, wide)
    put_in_order(out, matrix, made, first, per)


def put_in_order(out, base, total, first, per):
    height = out.shape[0]
    for other in range(per):

        @pl.when(first == other)
        def _():
            for t in range(per):
                here = slice(t * height, (t + 1) * height)
                there = slice((t ^ other) * height, ((t ^ other) + 1) * height)
                out[:, here] = base[:, here] + total[:, there]


def sides_kernel(near, matrix, out):
    refl = near[: matrix.shape[0], :]
    out[...] = pair_dot(halves(refl), halves(matrix[...]), DOWN)


def sum_kernel(per, *refs):
    *blocks, base, out, made = refs
    _, first = place_in_kernel(per)
    total = blocks[0][...]
    for block in blocks[1:]:
        total = total + block[...]
    made[...] = total
    put_in_order(out, base, made, first, per)


def late_kernel(passed, across, other, sides, beside, out, added):
    added[...] = sides[...] + beside[...]

    @pl.when(at_end())
    def _():
        out[...] = other[...]

    @pl.when(jnp.logical_not(at_end()))
    def _():
        out[...] = passed[...] + across[...]


def image_kernel(summed, sides, *refs):
    *parts, near, out = refs
    refl = near[: out.shape[0], :]
    whole = sides[...] + jnp.concatenate([part[...] for part in parts], axis=0)
    out[...] = summed[...] - pair_dot(halves(refl), halves(whole), OVER)


def last_kernel(per, summed, late, passed, out, made):
    _, first = place_in_kernel(per)
    made[...] = late[...]

    @pl.when(at_end())
    def _():
        made[...] = made[...] + passed[...]

    put_in_order(out, summed, made, first, per)


def run_kernel(body, outs, args, scratch=(), flops=0, moved=0):
    vmem = pl.BlockSpec(memory_space=pltpu.VMEM)
    return pl.pallas_call(
        body,
        out_shape=[jax.ShapeDtypeStruct(shape, jnp.float32) for shape in outs],
        in_specs=[vmem] * len(args),
        out_specs=[vmem] * len(outs),
        scratch_shapes=list(scratch),
        compiler_params=pltpu.CompilerParams(vmem_limit_bytes=VMEM_BYTES),
        cost_estimate=pl.CostEstimate(flops=flops, bytes_accessed=moved, transcendentals=0),
    )(*args)


def blocks_plain(panels, refls, matrix, base, first, cols, per):
    all_panels, all_refl = jnp.concatenate(panels, axis=0), jnp.concatenate(refls, axis=0)
    own, own_refl = panels[0], refls[0]
    height, share = own.shape[0], own.shape[1] // 2
    wide = per * height
    left_panel, right_panel = own[:, :share], own[:, share:]
    mixed = dot(all_panels, all_refl, DOWN)
    mixed_left, mixed_right = mixed[:share], mixed[share:]
    mine = order_blocks(matrix, per, first)
    col_refl = lax.dynamic_slice_in_dim(all_refl, base * wide, wide, 0)
    image = (
        dot(right_panel, mixed_left, OVER)
        - dot(left_panel, mixed_right, OVER)
        + dot(mine, col_refl, OVER)
    )
    factors = jnp.concatenate(
        [
            right_panel - dot(own_refl, mixed_right, ALONG),
            dot(own_refl, mixed_left, ALONG) - left_panel,
            -image,
        ],
        axis=1,
    )
    whole = jnp.concatenate([all_panels, all_refl], axis=1)
    return [
        dot(factors, lax.dynamic_slice_in_dim(whole, (base ^ k) * wide, wide, 0), ALONG)
        for k in range(cols)
    ]


def gather_columns(reflectors, cols):
    value, bit = reflectors, 1
    while bit < cols:
        value = jnp.concatenate([value, swap(value, "col", bit)], axis=1)
        bit *= 2
    return value


def local_square(matrix, left_panel, right_panel, reflectors):
    rows, cols = lax.axis_size("row"), lax.axis_size("col")
    per = rows // cols
    height, share = left_panel.shape
    wide = per * height
    refl_parts, bit = [reflectors.T], 1
    while bit < cols:
        known = jnp.concatenate(refl_parts, axis=0)
        refl_parts = [known, swap(known, "col", bit)]
        bit *= 2
    found, near, sides, by_x = gather_square(left_panel, right_panel, refl_parts, matrix)
    width = share
    sides, _ = lax.optimization_barrier((sides, by_x))
    beside = swap(sides, "row", 2)

    arrays = [value for value, _ in found]
    pieces = tuple(places for _, places in found)
    total, depth = rows * height, 2 * share + width
    halved = pltpu.VMEM((total, depth), jnp.bfloat16)
    block = pltpu.VMEM((height, wide), jnp.float32)
    order = tuple(range(0, rows, 2))
    mine = [n for n, places in enumerate(pieces) if all(i in order for i, _ in places)]
    known = pltpu.VMEM((len(order) * height, depth), jnp.bfloat16)
    mixed, image = run_kernel(
        functools.partial(mix_kernel, tuple(pieces[n] for n in mine), order, per, share),
        [(width, 2 * share), (height, width)],
        [arrays[n] for n in mine] + [matrix],
        [known, known],
        12 * len(order) * height * share * width,
        4 * len(order) * height * depth,
    )
    factors, *blocks = run_kernel(
        functools.partial(send_kernel, pieces, order, per, share),
        [(height, depth)] + [(height, wide)] * (cols - 1),
        arrays + [mixed, image, matrix],
        [halved, halved],
        12 * (total - len(order) * height) * share * width + 6 * total * height * depth,
        4 * total * depth,
    )
    received = [lax.ppermute(blocks[2], "col", [(1, 2), (2, 1)])]
    passed = swap(blocks[0], "col", 1)
    received += [lax.ppermute(blocks[1], "col", [(0, 2), (3, 1)])]
    late, sides = run_kernel(
        late_kernel,
        [(height, wide), (width, wide)],
        [passed, blocks[1], blocks[2], sides, beside],
    )
    late = lax.ppermute(late, "col", [(0, 1), (3, 2), (1, 3), (2, 0)])
    (base,) = run_kernel(
        functools.partial(keep_kernel, pieces, per, share),
        [(height, wide)],
        arrays + [factors, matrix],
        [halved, halved, block],
        6 * wide * height * depth,
        4 * total * depth,
    )
    parts = [swap(sides[n : n + width // 2], "row", 4) for n in (0, width // 2)]
    (summed,) = run_kernel(
        functools.partial(sum_kernel, per),
        [(height, wide)],
        [*received, base],
        [block],
        height * wide * cols,
        16 * height * wide * (cols + 1),
    )
    summed, parts = lax.optimization_barrier((summed, parts))
    (summed,) = run_kernel(
        image_kernel,
        [(height, wide)],
        [summed, sides, *parts, near],
        (),
        6 * height * width * wide,
        4 * width * wide * 2,
    )
    (updated,) = run_kernel(
        functools.partial(last_kernel, per),
        [(height, wide)],
        [summed, late, passed],
        [block],
        2 * height * wide,
        16 * height * wide,
    )
    return updated


def local_general(matrix, left_panel, right_panel, reflectors):
    rows, cols = lax.axis_size("row"), lax.axis_size("col")
    per = rows // cols
    row, col = lax.axis_index("row"), lax.axis_index("col")
    base, first = (row // per) ^ col, row % per
    own_refl = gather_columns(reflectors, cols)
    panels = gather_row(jnp.concatenate([left_panel, right_panel], axis=1), rows)
    refls = gather_row(own_refl, rows)
    made = blocks_plain(panels, refls, matrix, base, first, cols, per)
    total = made[0]
    for k in range(1, cols):
        total = total + swap(made[k], "col", k)
    sides = chips_sum(core_sum(dot(own_refl, matrix, DOWN)), rows)
    return order_blocks(total, per, first) + (matrix - dot(own_refl, sides, OVER))


def local(matrix, left_panel, right_panel, reflectors):
    rows, cols = lax.axis_size("row"), lax.axis_size("col")
    height, share = left_panel.shape
    width = reflectors.shape[1] * cols
    need = rows * height * (2 * share + width) * 8 + rows * height * height * 8
    if rows == 8 and cols == 4 and share == width and need <= VMEM_BYTES:
        return local_square(matrix, left_panel, right_panel, reflectors)
    return local_general(matrix, left_panel, right_panel, reflectors)


def solution(mesh):
    spec = P("row", "col")
    return jax.shard_map(
        local, mesh=mesh, in_specs=(spec,) * 4, out_specs=spec, check_vma=False
    )
```

```python
import functools

import jax
import jax.numpy as jnp
from jax import lax
from jax.experimental import pallas as pl
from jax.experimental.pallas import tpu as pltpu
from jax.sharding import PartitionSpec as P

ALONG = ((1,), (1,))
OVER = ((1,), (0,))
DOWN = ((0,), (0,))
VMEM_BYTES = 24 * 2**20


def dot(first, second, dims):
    return lax.dot_general(
        first,
        second,
        (dims, ((), ())),
        precision=lax.Precision.HIGH,
        preferred_element_type=jnp.float32,
    )


def halves(value):
    high = value.astype(jnp.bfloat16)
    return high, (value - high.astype(jnp.float32)).astype(jnp.bfloat16)


def pair_dot(first, second, dims):
    def one(a, b):
        return lax.dot_general(a, b, (dims, ((), ())), preferred_element_type=jnp.float32)

    return one(first[0], second[0]) + (one(first[0], second[1]) + one(first[1], second[0]))


def swap(value, axis, offset):
    size = lax.axis_size(axis)
    return lax.ppermute(value, axis, [(i, i ^ offset) for i in range(size)])


def gather_row(value, rows):
    blocks = []
    for chip in range(0, rows, 2):
        here = swap(value, "row", chip) if chip else value
        blocks += [here, swap(here, "row", 1)]
    return blocks


def stack(*parts):
    return jnp.concatenate(parts, axis=0)


def pack_kernel(left_x, right_x, left_y, right_y, *refs):
    *parts, by_x, by_y, near = refs
    height = left_x.shape[0]
    near[:height, :] = jnp.concatenate([part[...] for part in parts], axis=0).T
    for n, value in enumerate((left_x, right_x, left_y, right_y)):
        near[(n + 1) * height : (n + 2) * height, :] = value[...]
    by_x[:height, :] = left_y[...]
    by_x[height:, :] = near[:height, :]
    by_y[:height, :] = right_x[...]
    by_y[height:, :] = near[:height, :]


def gather_square(left_panel, right_panel, refl_parts, matrix):
    height, width = left_panel.shape
    wide = matrix.shape[1]
    near = [swap(panel, "row", bits) for bits in (2, 4) for panel in (left_panel, right_panel)]
    by_x, by_y, near = run_kernel(
        pack_kernel,
        [(2 * height, width)] * 2 + [(5 * height, width)],
        [*near, *refl_parts],
        (),
        0,
        72 * height * width,
    )
    far = swap(near[:height], "row", 6)
    by_x, by_y = swap(by_x, "row", 2), swap(by_y, "row", 4)
    (sides,) = run_kernel(
        sides_kernel,
        [(width, wide)],
        [near, matrix],
        (),
        6 * height * width * wide,
        4 * height * (width + wide),
    )
    across_sides = swap(sides, "row", 1)
    panels = stack(left_panel, right_panel)
    across_own = swap(panels, "row", 1)
    last, across_own, _ = lax.optimization_barrier(
        (stack(by_x, by_y, far), across_own, across_sides)
    )
    sides = sides + across_sides
    own_at = ((0, 0), (0, 1))
    near_at = ((0, 2), (2, 0), (2, 1), (4, 0), (4, 1))
    last_at = ((6, 0), (2, 2), (6, 1), (4, 2), (6, 2))

    def across(places):
        return tuple((index + 1, kind) for index, kind in places)

    found = [(panels, own_at), (across_own, across(own_at))]
    for value, places in ((near, near_at), (last, last_at)):
        found += [(value, places), (swap(value, "row", 1), across(places))]
    return found, near, sides, by_x


def core_sum(value):
    core = lax.axis_index("row") % 2
    half = value.shape[0] // 2
    kept = lax.dynamic_slice_in_dim(value, core * half, half, 0)
    given = lax.dynamic_slice_in_dim(value, (1 - core) * half, half, 0)
    return kept + swap(given, "row", 1)


def chips_sum(total, rows):
    bit = 2
    while bit < rows:
        total = total + swap(total, "row", bit)
        bit *= 2
    core = lax.axis_index("row") % 2
    other = swap(total, "row", 1)
    first = jnp.where(core == 0, total, other)
    second = jnp.where(core == 0, other, total)
    return jnp.concatenate([first, second], axis=0)


def order_blocks(value, per, first):
    width = value.shape[1] // per
    bit = 1
    while bit < per:
        parts = [value[:, t * width : (t + 1) * width] for t in range(per)]
        moved = jnp.concatenate([parts[t ^ bit] for t in range(per)], axis=1)
        value = jnp.where((first // bit) % 2 == 1, moved, value)
        bit *= 2
    return value


def place_in_kernel(per):
    row, col = lax.axis_index("row"), lax.axis_index("col")
    return (row // per) ^ col, row % per


def at_end():
    col = lax.axis_index("col")
    return (col == 0) | (col == lax.axis_size("col") - 1)


def split_pieces(pieces, in_refs, high, low, height, share):
    for ref, places in zip(in_refs, pieces):
        for n, (index, kind) in enumerate(places):
            upper, lower = halves(ref[n * height : (n + 1) * height, :])
            rows = slice(index * height, (index + 1) * height)
            columns = slice(kind * share, (kind + 1) * share)
            high[rows, columns] = upper
            low[rows, columns] = lower


def block_of(factors, high, low, begin, wide):
    height = factors.shape[0] // 2
    rows = pl.ds(pl.multiple_of(begin, 16), wide)

    def one(a, b):
        return lax.dot_general(a, b, (ALONG, ((), ())), preferred_element_type=jnp.float32)

    both = one(factors, high[rows, :])
    return both[:height] + (both[height:] + one(factors[:height], low[rows, :]))


def of_core(matrix, first, same):
    height = matrix.shape[0]
    return jnp.where((first == 0) == same, matrix[:, :height], matrix[:, height:])


def mix_kernel(pieces, order, per, share, *refs):
    count = len(pieces)
    in_refs, (matrix, mixed, image, high, low) = refs[:count], refs[count:]
    height = matrix.shape[0]
    for ref, places in zip(in_refs, pieces):
        for n, (index, kind) in enumerate(places):
            upper, lower = halves(ref[n * height : (n + 1) * height, :])
            rows = slice(order.index(index) * height, (order.index(index) + 1) * height)
            columns = slice(kind * share, (kind + 1) * share)
            high[rows, columns] = upper
            low[rows, columns] = lower
    panels = (high[:, : 2 * share], low[:, : 2 * share])
    refl = (high[:, 2 * share :], low[:, 2 * share :])
    mixed[...] = pair_dot(refl, panels, DOWN)
    base, first = place_in_kernel(per)
    rows = pl.ds(pl.multiple_of(base * height, 16), height)
    image[...] = pair_dot(
        halves(of_core(matrix, first, True)), (high[rows, 2 * share :], low[rows, 2 * share :]), OVER
    )


def send_kernel(pieces, order, per, share, *refs):
    count = len(pieces)
    in_refs, (mixed_ref, image_ref, matrix, factors_ref) = refs[:count], refs[count : count + 4]
    outs, (high, low) = refs[count + 4 : -2], refs[-2:]
    height = matrix.shape[0]
    wide = per * height
    base, first = place_in_kernel(per)
    split_pieces(pieces, in_refs, high, low, height, share)
    others = [index for index in range(high.shape[0] // height) if index not in order]

    def of_others(ref, columns):
        return jnp.concatenate(
            [ref[index * height : (index + 1) * height, columns] for index in others], axis=0
        )

    refl_at, panels_at = slice(2 * share, None), slice(0, 2 * share)
    mixed = mixed_ref[...] + pair_dot(
        (of_others(high, refl_at), of_others(low, refl_at)),
        (of_others(high, panels_at), of_others(low, panels_at)),
        DOWN,
    )
    mixed_pair = halves(mixed)
    left_panel, right_panel = in_refs[0][:height, :], in_refs[0][height:, :]
    own_refl = (high[:height, 2 * share :], low[:height, 2 * share :])
    rows = pl.ds(pl.multiple_of((base * per + 1) * height, 16), height)
    image = image_ref[...] + pair_dot(
        halves(of_core(matrix, first, False)),
        (high[rows, 2 * share :], low[rows, 2 * share :]),
        OVER,
    )
    spread = pair_dot(own_refl, mixed_pair, OVER)
    turned = halves(jnp.concatenate([right_panel, -left_panel], axis=1))
    image = image + pair_dot(turned, mixed_pair, ALONG)
    factors = jnp.concatenate(
        [right_panel - spread[:, share:], spread[:, :share] - left_panel, -image], axis=1
    )
    factors_ref[...] = factors
    stacked = jnp.concatenate(halves(factors), axis=0)
    onward = jnp.where(at_end(), 3, 1)
    for k, out in zip((onward, 2, 4 - onward), outs):
        out[...] = block_of(stacked, high, low, (base ^ k) * wide, wide)


def keep_kernel(pieces, per, share, *refs):
    count = len(pieces)
    in_refs, (factors_ref, matrix, out, high, low, made) = refs[:count], refs[count:]
    height = matrix.shape[0]
    wide = per * height
    base, first = place_in_kernel(per)
    split_pieces(pieces, in_refs, high, low, height, share)
    stacked = jnp.concatenate(halves(factors_ref[...]), axis=0)
    made[...] = block_of(stacked, high, low, base * wide, wide)
    put_in_order(out, matrix, made, first, per)


def put_in_order(out, base, total, first, per):
    height = out.shape[0]
    for other in range(per):

        @pl.when(first == other)
        def _():
            for t in range(per):
                here = slice(t * height, (t + 1) * height)
                there = slice((t ^ other) * height, ((t ^ other) + 1) * height)
                out[:, here] = base[:, here] + total[:, there]


def sides_kernel(near, matrix, out):
    refl = near[: matrix.shape[0], :]
    out[...] = pair_dot(halves(refl), halves(matrix[...]), DOWN)


def sum_kernel(per, *refs):
    *blocks, base, out, made = refs
    _, first = place_in_kernel(per)
    total = blocks[0][...]
    for block in blocks[1:]:
        total = total + block[...]
    made[...] = total
    put_in_order(out, base, made, first, per)


def late_kernel(passed, across, other, sides, beside, out, added):
    added[...] = sides[...] + beside[...]

    @pl.when(at_end())
    def _():
        out[...] = other[...]

    @pl.when(jnp.logical_not(at_end()))
    def _():
        out[...] = passed[...] + across[...]


def image_kernel(summed, sides, *refs):
    *parts, near, out = refs
    refl = near[: out.shape[0], :]
    whole = sides[...] + jnp.concatenate([part[...] for part in parts], axis=0)
    out[...] = summed[...] - pair_dot(halves(refl), halves(whole), OVER)


def last_kernel(per, summed, late, passed, out, made):
    _, first = place_in_kernel(per)
    made[...] = late[...]

    @pl.when(at_end())
    def _():
        made[...] = made[...] + passed[...]

    put_in_order(out, summed, made, first, per)


def run_kernel(body, outs, args, scratch=(), flops=0, moved=0):
    vmem = pl.BlockSpec(memory_space=pltpu.VMEM)
    return pl.pallas_call(
        body,
        out_shape=[jax.ShapeDtypeStruct(shape, jnp.float32) for shape in outs],
        in_specs=[vmem] * len(args),
        out_specs=[vmem] * len(outs),
        scratch_shapes=list(scratch),
        compiler_params=pltpu.CompilerParams(vmem_limit_bytes=VMEM_BYTES),
        cost_estimate=pl.CostEstimate(flops=flops, bytes_accessed=moved, transcendentals=0),
    )(*args)


def blocks_plain(panels, refls, matrix, base, first, cols, per):
    all_panels, all_refl = jnp.concatenate(panels, axis=0), jnp.concatenate(refls, axis=0)
    own, own_refl = panels[0], refls[0]
    height, share = own.shape[0], own.shape[1] // 2
    wide = per * height
    left_panel, right_panel = own[:, :share], own[:, share:]
    mixed = dot(all_panels, all_refl, DOWN)
    mixed_left, mixed_right = mixed[:share], mixed[share:]
    mine = order_blocks(matrix, per, first)
    col_refl = lax.dynamic_slice_in_dim(all_refl, base * wide, wide, 0)
    image = (
        dot(right_panel, mixed_left, OVER)
        - dot(left_panel, mixed_right, OVER)
        + dot(mine, col_refl, OVER)
    )
    factors = jnp.concatenate(
        [
            right_panel - dot(own_refl, mixed_right, ALONG),
            dot(own_refl, mixed_left, ALONG) - left_panel,
            -image,
        ],
        axis=1,
    )
    whole = jnp.concatenate([all_panels, all_refl], axis=1)
    return [
        dot(factors, lax.dynamic_slice_in_dim(whole, (base ^ k) * wide, wide, 0), ALONG)
        for k in range(cols)
    ]


def gather_columns(reflectors, cols):
    value, bit = reflectors, 1
    while bit < cols:
        value = jnp.concatenate([value, swap(value, "col", bit)], axis=1)
        bit *= 2
    return value


def local_square(matrix, left_panel, right_panel, reflectors):
    rows, cols = lax.axis_size("row"), lax.axis_size("col")
    per = rows // cols
    height, share = left_panel.shape
    wide = per * height
    refl_parts, bit = [reflectors.T], 1
    while bit < cols:
        known = jnp.concatenate(refl_parts, axis=0)
        refl_parts = [known, swap(known, "col", bit)]
        bit *= 2
    found, near, sides, by_x = gather_square(left_panel, right_panel, refl_parts, matrix)
    width = share
    sides, _ = lax.optimization_barrier((sides, by_x))
    beside = swap(sides, "row", 2)

    arrays = [value for value, _ in found]
    pieces = tuple(places for _, places in found)
    total, depth = rows * height, 2 * share + width
    halved = pltpu.VMEM((total, depth), jnp.bfloat16)
    block = pltpu.VMEM((height, wide), jnp.float32)
    order = tuple(range(0, rows, 2))
    mine = [n for n, places in enumerate(pieces) if all(i in order for i, _ in places)]
    known = pltpu.VMEM((len(order) * height, depth), jnp.bfloat16)
    mixed, image = run_kernel(
        functools.partial(mix_kernel, tuple(pieces[n] for n in mine), order, per, share),
        [(width, 2 * share), (height, width)],
        [arrays[n] for n in mine] + [matrix],
        [known, known],
        12 * len(order) * height * share * width,
        4 * len(order) * height * depth,
    )
    factors, *blocks = run_kernel(
        functools.partial(send_kernel, pieces, order, per, share),
        [(height, depth)] + [(height, wide)] * (cols - 1),
        arrays + [mixed, image, matrix],
        [halved, halved],
        12 * (total - len(order) * height) * share * width + 6 * total * height * depth,
        4 * total * depth,
    )
    passed = swap(blocks[0], "col", 1)
    received = [lax.ppermute(blocks[2], "col", [(1, 2), (2, 1)])]
    received += [lax.ppermute(blocks[1], "col", [(0, 2), (3, 1)])]
    late, sides = run_kernel(
        late_kernel,
        [(height, wide), (width, wide)],
        [passed, blocks[1], blocks[2], sides, beside],
    )
    late = lax.ppermute(late, "col", [(0, 1), (3, 2), (1, 3), (2, 0)])
    (base,) = run_kernel(
        functools.partial(keep_kernel, pieces, per, share),
        [(height, wide)],
        arrays + [factors, matrix],
        [halved, halved, block],
        6 * wide * height * depth,
        4 * total * depth,
    )
    parts = [swap(sides[n : n + width // 2], "row", 4) for n in (0, width // 2)]
    (summed,) = run_kernel(
        functools.partial(sum_kernel, per),
        [(height, wide)],
        [*received, base],
        [block],
        height * wide * cols,
        16 * height * wide * (cols + 1),
    )
    summed, parts = lax.optimization_barrier((summed, parts))
    (summed,) = run_kernel(
        image_kernel,
        [(height, wide)],
        [summed, sides, *parts, near],
        (),
        6 * height * width * wide,
        4 * width * wide * 2,
    )
    (updated,) = run_kernel(
        functools.partial(last_kernel, per),
        [(height, wide)],
        [summed, late, passed],
        [block],
        2 * height * wide,
        16 * height * wide,
    )
    return updated


def local_general(matrix, left_panel, right_panel, reflectors):
    rows, cols = lax.axis_size("row"), lax.axis_size("col")
    per = rows // cols
    row, col = lax.axis_index("row"), lax.axis_index("col")
    base, first = (row // per) ^ col, row % per
    own_refl = gather_columns(reflectors, cols)
    panels = gather_row(jnp.concatenate([left_panel, right_panel], axis=1), rows)
    refls = gather_row(own_refl, rows)
    made = blocks_plain(panels, refls, matrix, base, first, cols, per)
    total = made[0]
    for k in range(1, cols):
        total = total + swap(made[k], "col", k)
    sides = chips_sum(core_sum(dot(own_refl, matrix, DOWN)), rows)
    return order_blocks(total, per, first) + (matrix - dot(own_refl, sides, OVER))


def local(matrix, left_panel, right_panel, reflectors):
    rows, cols = lax.axis_size("row"), lax.axis_size("col")
    height, share = left_panel.shape
    width = reflectors.shape[1] * cols
    need = rows * height * (2 * share + width) * 8 + rows * height * height * 8
    if rows == 8 and cols == 4 and share == width and need <= VMEM_BYTES:
        return local_square(matrix, left_panel, right_panel, reflectors)
    return local_general(matrix, left_panel, right_panel, reflectors)


def solution(mesh):
    spec = P("row", "col")
    return jax.shard_map(
        local, mesh=mesh, in_specs=(spec,) * 4, out_specs=spec, check_vma=False
    )
```
